32 devices in a mesh: row: 4 (over y, x), col: 8 (over z, core).
Axes of the slice: x: 2, y: 2, z: 4, core: 2. Of those that a mesh axis runs over, the one named last changes fastest.
Arguments:
- object_field: float32 [2, 1536, 2048], P(None, 'row', 'col'), may hold values from -6 to 6
- probe_modes: float32 [2, 2, 128, 128], replicated, may hold values from -2.1 to 2.1
- measured: float32 [4, 8, 8, 128, 128], P('row', 'col'), may hold values from 0.1 to 3
- positions: int32 [4, 8, 2, 8], P('row', 'col'), may hold values from 0 to 383, as said below
- counts: int32 [4, 8], P('row', 'col'), may hold values from 2 to 8, as said below
Outputs:
- object_new: float32 [2, 1536, 2048], P(None, 'row', 'col')
- probe_step: float32 [2, 2, 128, 128], replicated
The draws below stay inside these ranges and needn't reach their ends.
Inputs may be any that keep to these rules, and one draw needn't show every extreme that they name: `positions`: offsets lie inside the tile: row offsets below 384, column offsets below 256; both edges are reached. `counts`: some tile uses all 8 slots.
All inputs are finite; a program needn't handle non-finite values.
Results may differ from the reference program's by a relative error of at most 0.0003.
Values sent between devices are 32-bit elements; how exact they have to be, the bound alone decides.
A program may use at most 64 MiB of HBM per device.

```python
import math
import jax
import jax.numpy as jnp
from jax import lax

PATCH = 128
MODES = 2
TILE_HEIGHT = 384
TILE_WIDTH = 256
SLOTS = 8
GRID_HEIGHT = 4
GRID_WIDTH = 8
OBJECT_HEIGHT = 1536
OBJECT_WIDTH = 2048


def draw_positions(key, part):
    down_offset = jax.random.randint(jax.random.fold_in(key, 11), (GRID_HEIGHT, GRID_WIDTH, SLOTS), 0, TILE_HEIGHT)
    side_offset = jax.random.randint(jax.random.fold_in(key, 12), (GRID_HEIGHT, GRID_WIDTH, SLOTS), 0, TILE_WIDTH)
    down_offset = down_offset.at[0, 0, 0].set(TILE_HEIGHT - 1).at[0, 0, 1].set(0)
    side_offset = side_offset.at[0, 0, 0].set(TILE_WIDTH - 1).at[0, 0, 1].set(0)
    return jnp.stack([down_offset, side_offset], axis=2).astype(jnp.int32)


def draw_counts(key, part):
    tiles = GRID_HEIGHT * GRID_WIDTH
    spread = jax.random.randint(jax.random.fold_in(key, 21), (tiles,), 0, SLOTS - 1)
    filled = 2 + spread * spread // max(SLOTS - 2, 1)
    chosen = jax.random.randint(jax.random.fold_in(key, 22), (), 0, tiles)
    filled = jnp.where(jnp.arange(tiles, dtype=jnp.int32) == chosen, SLOTS, filled)
    return filled.reshape(GRID_HEIGHT, GRID_WIDTH).astype(jnp.int32)


def block_levels(own_key, shape, cuts, smallest, top_value):
    factor_of = 1.0
    for dim, parts in cuts:
        steps = jax.random.uniform(jax.random.fold_in(jax.random.fold_in(own_key, 6), dim), (parts,), jnp.float32, smallest / len(cuts), top_value / len(cuts))
        factor_of = factor_of * jnp.repeat(jnp.exp(steps), shape[dim] // parts).reshape((-1,) + (1,) * (len(shape) - 1 - dim))
    return factor_of


def bell_draw(rng, extent, deviation, most, pieces=(), kind=jnp.bfloat16):
    values = jax.random.normal(rng, extent, jnp.float32) * deviation
    if len(pieces) > 0:
        values = block_levels(rng, extent, pieces, -0.22, 0.18) * values
    return jnp.clip(values, min=-most, max=most).astype(kind)


def setup_inputs(seed: int = 0) -> dict:
    keys = jax.random.split(jax.random.key(seed), 6)
    return {
        "object_field": bell_draw(keys[0], (2, OBJECT_HEIGHT, OBJECT_WIDTH), 1.0, 6.0, ((1, 4), (2, 8)), jnp.float32),
        "probe_modes": bell_draw(keys[1], (2, MODES, PATCH, PATCH), 0.35, 2.1, (), jnp.float32),
        "measured": jnp.clip(jnp.exp(math.log(3.0) - 3.4011974 * jax.random.uniform(keys[2], (GRID_HEIGHT, GRID_WIDTH, SLOTS, PATCH, PATCH), jnp.float32) ** block_levels(keys[2], (GRID_HEIGHT, GRID_WIDTH, SLOTS, PATCH, PATCH), ((0, 4), (1, 8)), -0.2, 0.2)), 0.1, 3.0),
        "positions": draw_positions(jax.random.fold_in(keys[5], 71), 0),
        "counts": draw_counts(jax.random.fold_in(keys[5], 71), 0),
    }


HIGHEST = lax.Precision.HIGHEST
AMP_FLOOR = 0.25

def fourier_tables(patch_width):
    index = jnp.arange(patch_width, dtype=jnp.int32)
    product = index[:, None] * index[None, :] % patch_width
    angle = product.astype(jnp.float32) * (2.0 * math.pi / patch_width)
    scale = 1.0 / math.sqrt(patch_width)
    return (jnp.cos(angle) * scale, jnp.sin(angle) * scale)

def transform(real_part, imag_part, cosine_table, sine_table, sign_value):
    left_real = jnp.einsum('jk,...kl->...jl', cosine_table, real_part, precision=HIGHEST) - sign_value * jnp.einsum('jk,...kl->...jl', sine_table, imag_part, precision=HIGHEST)
    left_imag = jnp.einsum('jk,...kl->...jl', cosine_table, imag_part, precision=HIGHEST) + sign_value * jnp.einsum('jk,...kl->...jl', sine_table, real_part, precision=HIGHEST)
    out_real = jnp.einsum('...jk,kl->...jl', left_real, cosine_table, precision=HIGHEST) - sign_value * jnp.einsum('...jk,kl->...jl', left_imag, sine_table, precision=HIGHEST)
    out_imag = jnp.einsum('...jk,kl->...jl', left_imag, cosine_table, precision=HIGHEST) + sign_value * jnp.einsum('...jk,kl->...jl', left_real, sine_table, precision=HIGHEST)
    return (out_real, out_imag)

def contributions(patches, probe_modes, amplitudes, live_slots, cosine_table, sine_table):
    patch_real = patches[:, 0][:, None]
    patch_imag = patches[:, 1][:, None]
    mode_real = probe_modes[0][None]
    mode_imag = probe_modes[1][None]
    exit_real = mode_real * patch_real - mode_imag * patch_imag
    exit_imag = mode_real * patch_imag + mode_imag * patch_real
    far_real, far_imag = transform(exit_real, exit_imag, cosine_table, sine_table, -1.0)
    intensity = lax.optimization_barrier(jnp.sum(far_real * far_real + far_imag * far_imag, axis=1))
    scaling = (amplitudes / jnp.maximum(jnp.sqrt(intensity), AMP_FLOOR) - 1.0) * live_slots[:, None, None]
    scaling = scaling[:, None]
    back_real, back_imag = transform(far_real * scaling, far_imag * scaling, cosine_table, sine_table, 1.0)
    object_real = lax.optimization_barrier(jnp.sum(mode_real * back_real + mode_imag * back_imag, axis=1))
    object_imag = lax.optimization_barrier(jnp.sum(mode_real * back_imag - mode_imag * back_real, axis=1))
    probe_real = lax.optimization_barrier(jnp.sum(patch_real * back_real + patch_imag * back_imag, axis=0))
    probe_imag = lax.optimization_barrier(jnp.sum(patch_real * back_imag - patch_imag * back_real, axis=0))
    density = lax.optimization_barrier(jnp.sum(live_slots[:, None, None] * (patches[:, 0] * patches[:, 0] + patches[:, 1] * patches[:, 1]), axis=0))
    return (jnp.stack([object_real, object_imag], axis=1), jnp.stack([probe_real, probe_imag]), density)

def cut_patches(field, row_starts, col_starts, patch_width):

    def one_patch(row_start, col_start):
        return lax.dynamic_slice(field, (jnp.int32(0), row_start, col_start), (2, patch_width, patch_width))
    return jax.vmap(one_patch)(row_starts.astype(jnp.int32), col_starts.astype(jnp.int32))

def accumulate(gradient, object_terms, row_starts, col_starts):
    patch_width = object_terms.shape[-1]

    def add_one(slot_index, totals):
        corner_at = (jnp.int32(0), row_starts[slot_index].astype(jnp.int32), col_starts[slot_index].astype(jnp.int32))
        current = lax.dynamic_slice(totals, corner_at, (2, patch_width, patch_width))
        return lax.dynamic_update_slice(totals, current + object_terms[slot_index], corner_at)
    return lax.fori_loop(0, object_terms.shape[0], add_one, gradient)

def reference(object_field, probe_modes, measured, positions, counts):
    patch_width = probe_modes.shape[-1]
    capacity = positions.shape[-1]
    grid_height, grid_width = counts.shape
    object_height, object_width = (object_field.shape[1], object_field.shape[2])
    tile_height = object_height // grid_height
    tile_width = object_width // grid_width
    cosine_table, sine_table = fourier_tables(patch_width)
    padded = jnp.pad(object_field, ((0, 0), (0, patch_width), (0, patch_width)))
    tiles = grid_height * grid_width
    base_rows = jnp.broadcast_to((jnp.arange(grid_height, dtype=jnp.int32) * tile_height)[:, None], (grid_height, grid_width)).reshape(tiles)
    base_cols = jnp.broadcast_to((jnp.arange(grid_width, dtype=jnp.int32) * tile_width)[None, :], (grid_height, grid_width)).reshape(tiles)
    row_offsets = positions[:, :, 0, :].reshape(tiles, capacity).astype(jnp.int32)
    col_offsets = positions[:, :, 1, :].reshape(tiles, capacity).astype(jnp.int32)
    live_all = (jnp.arange(capacity, dtype=jnp.int32)[None, :] < counts.reshape(tiles, 1)).astype(jnp.float32)
    amplitude_all = measured.reshape(tiles, capacity, patch_width, patch_width)

    def device_step(totals, inputs_now):
        gradient, probe_sum, density_sum = totals
        base_row, base_col, row_part, col_part, live_slots, amplitudes = inputs_now
        row_starts = row_part + base_row
        col_starts = col_part + base_col
        patches = cut_patches(padded, row_starts, col_starts, patch_width)
        object_terms, probe_terms, density = contributions(patches, probe_modes, amplitudes, live_slots, cosine_table, sine_table)
        gradient = accumulate(gradient, object_terms, row_starts, col_starts)
        return ((gradient, probe_sum + probe_terms, density_sum + density), None)
    initial = (jnp.zeros_like(padded), jnp.zeros_like(probe_modes), jnp.zeros((patch_width, patch_width), jnp.float32))
    (gradient, probe_sum, density_sum), _ = lax.scan(device_step, initial, (base_rows, base_cols, row_offsets, col_offsets, live_all, amplitude_all))
    peak_power = jnp.max(lax.optimization_barrier(jnp.sum(probe_modes * probe_modes, axis=(0, 1))))
    object_new = object_field + gradient[:, :object_height, :object_width] / (peak_power + 1e-06)
    probe_step = probe_sum / jnp.sqrt(density_sum + 1.0)[None, None]
    return (object_new, probe_step)
```

```python
import functools
import math

import jax
import jax.numpy as jnp
import ml_dtypes
import numpy as np
from jax import lax
from jax.experimental import pallas as pl
from jax.experimental.pallas import tpu as pltpu
from jax.sharding import PartitionSpec as P

AMP_FLOOR = 0.25
F32 = jnp.float32
MESH = pl.DeviceIdType.MESH
VMEM = pl.BlockSpec(memory_space=pltpu.VMEM)
SMEM = pl.BlockSpec(memory_space=pltpu.SMEM)
LIMIT = 48 * 1024 * 1024


def fourier_tables(n):
    index = np.arange(n)
    angle = (index[:, None] * index[None, :] % n) * (2.0 * math.pi / n)
    c = np.cos(angle) / math.sqrt(n)
    s = np.sin(angle) / math.sqrt(n)
    a = np.block([[c, -s], [s, c]]).astype(np.float32)
    parts = []
    for w in (a, a.T):
        hi = w.astype(ml_dtypes.bfloat16)
        lo = (w - hi.astype(np.float32)).astype(ml_dtypes.bfloat16)
        parts += [hi, lo]
    return np.stack(parts)


def split(x):
    hi = x.astype(jnp.bfloat16)
    return hi, (x - hi.astype(F32)).astype(jnp.bfloat16)


def dot(a, b):
    return jnp.dot(a, b, preferred_element_type=F32)


def left(w_hi, w_lo, x):
    hi, lo = split(x)
    return dot(w_hi, hi) + (dot(w_hi, lo) + dot(w_lo, hi))


def right(x, w_hi, w_lo):
    hi, lo = split(x)
    return dot(hi, w_hi) + (dot(lo, w_hi) + dot(hi, w_lo))


def swap_blocks(x, n):
    return jnp.concatenate(
        [
            jnp.concatenate([x[:n, :n], x[n:, :n]], axis=1),
            jnp.concatenate([x[:n, n:], x[n:, n:]], axis=1),
        ],
        axis=0,
    )


def tiling(nrow, ncol, n):
    tiles = 5 * (n // 8)
    share = -(-tiles // nrow)
    part = -(-share // ncol)
    return tiles, share, part


def place():
    return lax.axis_index("row"), lax.axis_index("col")


def halo_kernel(nrow, ncol, n, obj_ref, ext_ref, send_sem, recv_sem):
    _, height, width = obj_ref.shape
    r, c = place()
    up, down = lax.rem(r + nrow - 1, nrow), lax.rem(r + 1, nrow)
    west, east = lax.rem(c + ncol - 1, ncol), lax.rem(c + 1, ncol)
    barrier = pltpu.get_barrier_semaphore()
    for peer in ((up, c), (down, c), (r, west), (r, east), (up, west), (down, east)):
        pl.semaphore_signal(barrier, inc=1, device_id=peer, device_id_type=MESH)
    pl.semaphore_wait(barrier, 6)

    def copy(index, src, dst, peer):
        return pltpu.make_async_remote_copy(
            src_ref=src,
            dst_ref=dst,
            send_sem=send_sem.at[index],
            recv_sem=recv_sem.at[index],
            device_id=peer,
            device_id_type=MESH,
        )

    blocks = width // n
    right_halo = ext_ref.at[:, blocks, :height]
    corner_halo = ext_ref.at[:, blocks, height:]
    copies = [
        (copy(0, obj_ref.at[:, :, :n], right_halo, (r, west)), c > 0, c < ncol - 1, right_halo),
        (
            copy(1, obj_ref.at[:, :n, :n], corner_halo, (up, west)),
            (r > 0) & (c > 0),
            (r < nrow - 1) & (c < ncol - 1),
            corner_halo,
        ),
    ]
    for b in range(blocks):
        halo = ext_ref.at[:, b, height:]
        source = obj_ref.at[:, :n, b * n : (b + 1) * n]
        copies.append((copy(2 + b, source, halo, (up, c)), r > 0, r < nrow - 1, halo))
    for one, sends, _, _ in copies:

        @pl.when(sends)
        def _():
            one.start()

    for b in range(blocks):
        ext_ref[:, b, :height] = obj_ref[:, :, b * n : (b + 1) * n]
    for one, sends, takes, halo in copies:

        @pl.when(jnp.logical_not(takes))
        def _():
            halo[...] = jnp.zeros(halo.shape, F32)

        @pl.when(takes)
        def _():
            one.wait_recv()

        @pl.when(sends)
        def _():
            one.wait_send()


def compute_kernel(
    shares, height, width, pos_ref, cnt_ref, ext_ref, probe_ref, meas_ref, table_ref, grad_ref, red_ref, sums
):
    n = probe_ref.shape[-1]
    slots = meas_ref.shape[0]
    tiles, share, padded = shares
    a_hi, a_lo, b_hi, b_lo = (table_ref[i] for i in range(4))
    pr = [probe_ref[0, 0], probe_ref[0, 1]]
    pi = [probe_ref[1, 0], probe_ref[1, 1]]
    power = pr[0] * pr[0] + pi[0] * pi[0] + (pr[1] * pr[1] + pi[1] * pi[1])
    inverse = 1.0 / (jnp.max(power, keepdims=True) + 1e-06)
    lane = lax.broadcasted_iota(jnp.int32, (n, n), 1)
    blocks = width // n
    grad_ref[...] = jnp.zeros(grad_ref.shape, F32)
    grad_ref[:, :blocks, :height] = ext_ref[:, :blocks, :height]
    sums[...] = jnp.zeros(sums.shape, F32)

    def one_slot(s, carry):
        row, col = pos_ref[0, s], pos_ref[1, s]
        live = jnp.where(s < cnt_ref[0, 0], 1.0, 0.0).astype(F32)
        near = col // n
        shift = lax.rem(col, n)
        back_shift = lax.rem(n - shift, n)
        rows = pl.ds(row, n)

        def cut(part):
            a = pltpu.roll(ext_ref[part, near, rows], back_shift, 1)
            b = pltpu.roll(ext_ref[part, near + 1, rows], back_shift, 1)
            return jnp.where(lane < n - shift, a, b)

        qr, qi = cut(0), cut(1)
        waves = jnp.concatenate(
            [
                jnp.concatenate([pr[m] * qr - pi[m] * qi for m in range(2)], axis=1),
                jnp.concatenate([pr[m] * qi + pi[m] * qr for m in range(2)], axis=1),
            ],
            axis=0,
        )
        far = right(swap_blocks(left(b_hi, b_lo, waves), n), a_hi, a_lo)
        squares = far * far
        intensity = squares[:n, :n] + squares[:n, n:] + (squares[n:, :n] + squares[n:, n:])
        scaling = (meas_ref[s] * lax.rsqrt(jnp.maximum(intensity, AMP_FLOOR * AMP_FLOOR)) - 1.0) * live
        scaling = jnp.concatenate([scaling, scaling], axis=1)
        scaling = jnp.concatenate([scaling, scaling], axis=0)
        back = left(a_hi, a_lo, swap_blocks(right(far * scaling, b_hi, b_lo), n))
        br = [back[:n, :n], back[:n, n:]]
        bi = [back[n:, :n], back[n:, n:]]
        for m in range(2):
            sums[m] += qr * br[m] + qi * bi[m]
            sums[2 + m] += qr * bi[m] - qi * br[m]
        sums[4] += live * (qr * qr + qi * qi)
        terms = (
            pr[0] * br[0] + pi[0] * bi[0] + (pr[1] * br[1] + pi[1] * bi[1]),
            pr[0] * bi[0] - pi[0] * br[0] + (pr[1] * bi[1] - pi[1] * br[1]),
        )
        for part in range(2):
            term = pltpu.roll(terms[part] * inverse, shift, 1)
            grad_ref[part, near, rows] += jnp.where(lane >= shift, term, 0.0)
            grad_ref[part, near + 1, rows] += jnp.where(lane < shift, term, 0.0)
        return carry

    lax.fori_loop(0, slots, one_slot, 0)
    per = n // 8
    if padded > share or share * red_ref.shape[0] > tiles:
        red_ref[...] = jnp.zeros(red_ref.shape, F32)
    for g in range(tiles):
        red_ref[g // share, g % share] = sums[g // per, 8 * (g % per) : 8 * (g % per) + 8]


def finish_kernel(
    nrow, ncol, n, shares,
    grad_ref, red_ref, obj_ref, probe_ref,
    got1, acc1, got2, acc2, all2, all1, in_right, in_below, in_corner,
    send1, recv1, send2, recv2, send3, recv3, send4, recv4, send_halo, recv_halo,
):
    _, height, width = obj_ref.shape
    tiles, share, part = shares
    blocks = width // n
    r, c = place()
    up, down = lax.rem(r + nrow - 1, nrow), lax.rem(r + 1, nrow)
    west, east = lax.rem(c + ncol - 1, ncol), lax.rem(c + 1, ncol)
    row_peer = lambda d: (lax.rem(r + d, nrow), c)
    col_peer = lambda d: (r, lax.rem(c + d, ncol))
    barrier = pltpu.get_barrier_semaphore()
    peers = [row_peer(d) for d in range(1, nrow)] + [col_peer(d) for d in range(1, ncol)]
    for peer in peers + [(up, west), (down, east)]:
        pl.semaphore_signal(barrier, inc=1, device_id=peer, device_id_type=MESH)
    pl.semaphore_wait(barrier, nrow + ncol)

    def copy(src, dst, send_sem, recv_sem, peer):
        return pltpu.make_async_remote_copy(
            src_ref=src,
            dst_ref=dst,
            send_sem=send_sem,
            recv_sem=recv_sem,
            device_id=peer,
            device_id_type=MESH,
        )

    first = []
    for d in range(1, nrow):
        peer = row_peer(d)
        first.append(copy(red_ref.at[peer[0]], got1.at[r], send1.at[d], recv1.at[d], peer))
        first[-1].start()

    spills = (
        (copy(grad_ref.at[:, blocks, :height], in_right, send_halo.at[0], recv_halo.at[0], (r, east)), c < ncol - 1, c > 0),
        (copy(grad_ref.at[:, :blocks, height:], in_below, send_halo.at[1], recv_halo.at[1], (down, c)), r < nrow - 1, r > 0),
        (
            copy(grad_ref.at[:, blocks, height:], in_corner, send_halo.at[2], recv_halo.at[2], (down, east)),
            (r < nrow - 1) & (c < ncol - 1),
            (r > 0) & (c > 0),
        ),
    )
    for one, sends, _ in spills:

        @pl.when(sends)
        def _():
            one.start()

    for b in range(blocks):
        obj_ref[:, :, b * n : (b + 1) * n] = grad_ref[:, b, :height]

    for one in first:
        one.wait_recv()
    total = red_ref[r]
    for d in range(1, nrow):
        total = total + got1[lax.rem(r + nrow - d, nrow)]
    acc1[...] = total.reshape(acc1.shape)

    second = []
    for d in range(1, ncol):
        peer = col_peer(d)
        second.append(copy(acc1.at[peer[1]], got2.at[c], send2.at[d], recv2.at[d], peer))
        second[-1].start()
    for one in second:
        one.wait_recv()
    total = acc1[c]
    for d in range(1, ncol):
        total = total + got2[lax.rem(c + ncol - d, ncol)]
    acc2[...] = total

    third = []
    for d in range(1, ncol):
        third.append(copy(acc2, all2.at[c], send3.at[d], recv3.at[d], col_peer(d)))
        third[-1].start()
    all2[c] = total

    for (one, _, takes), got in zip(spills, (in_right, in_below, in_corner)):

        @pl.when(takes)
        def _():
            one.wait_recv()
            if got is in_right:
                obj_ref[:, :, :n] += got[...]
            elif got is in_corner:
                obj_ref[:, :n, :n] += got[...]
            else:
                for b in range(blocks):
                    obj_ref[:, :n, b * n : (b + 1) * n] += got[:, b]

    for one in third:
        one.wait_recv()

    fourth = []
    for d in range(1, nrow):
        fourth.append(copy(all2, all1.at[r], send4.at[d], recv4.at[d], row_peer(d)))
        fourth[-1].start()
    all1[r] = all2[...]
    for one in fourth:
        one.wait_recv()

    per = n // 8

    def tile(g):
        k = g % share
        return all1[g // share, k // part, k % part]

    for i in range(per):
        factor = lax.rsqrt(tile(4 * per + i) + 1.0)
        for ch in range(4):
            probe_ref[ch // 2, ch % 2, 8 * i : 8 * i + 8] = tile(ch * per + i) * factor

    for one in first + second + third + fourth:
        one.wait_send()
    for one, sends, _ in spills:

        @pl.when(sends)
        def _():
            one.wait_send()


def per_device(nrow, ncol, table, object_field, probe_modes, measured, positions, counts):
    n = probe_modes.shape[-1]
    _, height, width = object_field.shape
    tiles, share, part = tiling(nrow, ncol, n)
    params = functools.partial(pltpu.CompilerParams, vmem_limit_bytes=LIMIT)
    extended = pl.pallas_call(
        functools.partial(halo_kernel, nrow, ncol, n),
        out_shape=jax.ShapeDtypeStruct((2, width // n + 1, height + n, n), F32),
        in_specs=[VMEM],
        out_specs=VMEM,
        scratch_shapes=[pltpu.SemaphoreType.DMA((2 + width // n,))] * 2,
        compiler_params=params(collective_id=0, has_side_effects=True),
    )(object_field)
    gradient, sums = pl.pallas_call(
        functools.partial(compute_kernel, (tiles, share, ncol * part), height, width),
        out_shape=(
            jax.ShapeDtypeStruct((2, width // n + 1, height + n, n), F32),
            jax.ShapeDtypeStruct((nrow, ncol * part, 8, n), F32),
        ),
        in_specs=[SMEM, SMEM, VMEM, VMEM, VMEM, VMEM],
        out_specs=(VMEM, VMEM),
        scratch_shapes=[pltpu.VMEM((5, n, n), F32)],
        compiler_params=params(),
    )(positions[0, 0], counts, extended, probe_modes, measured[0, 0], table)
    dma = pltpu.SemaphoreType.DMA
    return pl.pallas_call(
        functools.partial(finish_kernel, nrow, ncol, n, (tiles, share, part)),
        out_shape=(
            jax.ShapeDtypeStruct((2, height, width), F32),
            jax.ShapeDtypeStruct((2, 2, n, n), F32),
        ),
        in_specs=[VMEM, VMEM],
        out_specs=(VMEM, VMEM),
        scratch_shapes=[
            pltpu.VMEM((nrow, ncol * part, 8, n), F32),
            pltpu.VMEM((ncol, part, 8, n), F32),
            pltpu.VMEM((ncol, part, 8, n), F32),
            pltpu.VMEM((part, 8, n), F32),
            pltpu.VMEM((ncol, part, 8, n), F32),
            pltpu.VMEM((nrow, ncol, part, 8, n), F32),
            pltpu.VMEM((2, height, n), F32),
            pltpu.VMEM((2, width // n, n, n), F32),
            pltpu.VMEM((2, n, n), F32),
        ]
        + [dma((k,)) for k in (nrow, nrow, ncol, ncol, ncol, ncol, nrow, nrow, 3, 3)],
        compiler_params=params(collective_id=1, has_side_effects=True),
    )(gradient, sums)


def solution(mesh):
    nrow, ncol = mesh.shape["row"], mesh.shape["col"]
    in_specs = (
        P(None, "row", "col"),
        P(),
        P("row", "col", None, None, None),
        P("row", "col", None, None),
        P("row", "col"),
    )
    out_specs = (P(None, "row", "col"), P())

    def run(object_field, probe_modes, measured, positions, counts):
        table = jnp.asarray(fourier_tables(probe_modes.shape[-1]))
        return jax.shard_map(
            functools.partial(per_device, nrow, ncol, table),
            mesh=mesh, in_specs=in_specs, out_specs=out_specs, check_vma=False,
        )(object_field, probe_modes, measured, positions, counts)

    return run
```

```python
import functools
import math

import jax
import jax.numpy as jnp
import ml_dtypes
import numpy as np
from jax import lax
from jax.experimental import pallas as pl
from jax.experimental.pallas import tpu as pltpu
from jax.sharding import PartitionSpec as P

AMP_FLOOR = 0.25
F32 = jnp.float32
MESH = pl.DeviceIdType.MESH
VMEM = pl.BlockSpec(memory_space=pltpu.VMEM)
SMEM = pl.BlockSpec(memory_space=pltpu.SMEM)
LIMIT = 48 * 1024 * 1024


def fourier_tables(n):
    index = np.arange(n)
    angle = (index[:, None] * index[None, :] % n) * (2.0 * math.pi / n)
    c = np.cos(angle) / math.sqrt(n)
    s = np.sin(angle) / math.sqrt(n)
    a = np.block([[c, -s], [s, c]]).astype(np.float32)
    on_left, on_right = [], []
    for w in (a, a.T):
        hi = w.astype(ml_dtypes.bfloat16)
        lo = (w - hi.astype(np.float32)).astype(ml_dtypes.bfloat16)
        on_left.append(np.concatenate([hi, lo, hi], axis=1))
        on_right.append(np.concatenate([hi, lo, hi], axis=0))
    return np.stack(on_left), np.stack(on_right)


def split(x):
    hi = x.astype(jnp.bfloat16)
    return hi, (x - hi.astype(F32)).astype(jnp.bfloat16)


def left(table, x):
    hi, lo = split(x)
    return jnp.dot(table, jnp.concatenate([hi, hi, lo], axis=0), preferred_element_type=F32)


def right(x, table):
    hi, lo = split(x)
    return jnp.dot(jnp.concatenate([hi, hi, lo], axis=1), table, preferred_element_type=F32)


def swap_blocks(x, n):
    return jnp.concatenate(
        [
            jnp.concatenate([x[:n, :n], x[n:, :n]], axis=1),
            jnp.concatenate([x[:n, n:], x[n:, n:]], axis=1),
        ],
        axis=0,
    )


def tiling(nrow, n):
    tiles = 5 * (n // 8)
    half = -(-tiles // 2)
    return tiles, half, -(-half // nrow)


def place():
    return lax.axis_index("row"), lax.axis_index("col")


def remote(src, dst, send_sem, recv_sem, peer):
    return pltpu.make_async_remote_copy(
        src_ref=src, dst_ref=dst, send_sem=send_sem, recv_sem=recv_sem, device_id=peer, device_id_type=MESH
    )


def halo_kernel(nrow, ncol, n, obj_ref, ext_ref, send_sem, recv_sem, own_sem):
    _, height, width = obj_ref.shape
    blocks = width // n
    r, c = place()
    up, down = lax.rem(r + nrow - 1, nrow), lax.rem(r + 1, nrow)
    west, east = lax.rem(c + ncol - 1, ncol), lax.rem(c + 1, ncol)
    own = [
        pltpu.make_async_copy(obj_ref.at[:, :, b * n : (b + 1) * n], ext_ref.at[:, b, :height], own_sem.at[b])
        for b in range(blocks)
    ]
    barrier = pltpu.get_barrier_semaphore()
    for peer in ((up, c), (down, c), (r, west), (r, east)):
        pl.semaphore_signal(barrier, inc=1, device_id=peer, device_id_type=MESH)
    pl.semaphore_wait(barrier, 4)

    below = []
    for b in range(blocks):
        source = obj_ref.at[:, :n, b * n : (b + 1) * n]
        below.append(remote(source, ext_ref.at[:, b, height:], send_sem.at[b], recv_sem.at[b], (up, c)))
    right_halo = ext_ref.at[:, blocks, :height]
    corner_halo = ext_ref.at[:, blocks, height:]
    beside = remote(
        obj_ref.at[:, :, :n], right_halo, send_sem.at[blocks], recv_sem.at[blocks], (r, west)
    )
    corner = remote(
        ext_ref.at[:, 0, height:], corner_halo, send_sem.at[blocks + 1], recv_sem.at[blocks + 1], (r, west)
    )
    has_below, has_right = r < nrow - 1, c < ncol - 1

    @pl.when(r > 0)
    def _():
        below[0].start()

    @pl.when(c > 0)
    def _():
        beside.start()

    @pl.when(r > 0)
    def _():
        for one in below[1:]:
            one.start()

    for one in own:
        one.start()

    @pl.when(jnp.logical_not(has_below))
    def _():
        ext_ref[:, :, height:] = jnp.zeros((2, blocks + 1, n, n), F32)

    @pl.when(jnp.logical_not(has_right))
    def _():
        ext_ref[:, blocks, :] = jnp.zeros((2, height + n, n), F32)

    @pl.when(has_below)
    def _():
        below[0].wait_recv()

        @pl.when(c > 0)
        def _():
            corner.start()

        for one in below[1:]:
            one.wait_recv()

    for one in own:
        one.wait()

    @pl.when(has_right)
    def _():
        beside.wait_recv()

        @pl.when(has_below)
        def _():
            corner.wait_recv()

    @pl.when(r > 0)
    def _():
        for one in below:
            one.wait_send()

    @pl.when(c > 0)
    def _():
        beside.wait_send()

        @pl.when(has_below)
        def _():
            corner.wait_send()


def compute_kernel(
    shares, group, height, width,
    pos_ref, cnt_ref, ext_ref, probe_ref, meas_ref, left_ref, right_ref, grad_ref, red_ref, sums,
):
    n = probe_ref.shape[-1]
    slots = meas_ref.shape[0]
    tiles, half, share = shares
    blocks = width // n
    pr = [probe_ref[0, 0], probe_ref[0, 1]]
    pi = [probe_ref[1, 0], probe_ref[1, 1]]
    power = pr[0] * pr[0] + pi[0] * pi[0] + (pr[1] * pr[1] + pi[1] * pi[1])
    inverse = 1.0 / (jnp.max(power, keepdims=True) + 1e-06)
    lane = lax.broadcasted_iota(jnp.int32, (n, n), 1)
    grad_ref[...] = jnp.zeros(grad_ref.shape, F32)
    grad_ref[:, :blocks, :height] = ext_ref[:, :blocks, :height]
    sums[...] = jnp.zeros(sums.shape, F32)

    def some_slots(first, carry):
        pr = [probe_ref[0, 0], probe_ref[0, 1]]
        pi = [probe_ref[1, 0], probe_ref[1, 1]]
        numbers = [first * group + k for k in range(group)]
        starts, cuts, lefts = [], [], []
        for s in numbers:
            row, col = pos_ref[0, s], pos_ref[1, s]
            near = col // n
            shift = lax.rem(col, n)
            back_shift = lax.rem(n - shift, n)
            rows = pl.ds(row, n)
            starts.append((rows, near, shift))
            patch = []
            for part in range(2):
                a = pltpu.roll(ext_ref[part, near, rows], back_shift, 1)
                b = pltpu.roll(ext_ref[part, near + 1, rows], back_shift, 1)
                patch.append(jnp.where(lane < n - shift, a, b))
            cuts.append(patch)
            qr, qi = patch
            waves = jnp.concatenate(
                [
                    jnp.concatenate([pr[m] * qr - pi[m] * qi for m in range(2)], axis=1),
                    jnp.concatenate([pr[m] * qi + pi[m] * qr for m in range(2)], axis=1),
                ],
                axis=0,
            )
            lefts.append(swap_blocks(left(left_ref[1], waves), n))
        far = right(jnp.concatenate(lefts, axis=0), right_ref[0])
        scaled = []
        for k, s in enumerate(numbers):
            live = jnp.where(s < cnt_ref[0, 0], 1.0, 0.0).astype(F32)
            mine = far[2 * n * k : 2 * n * (k + 1)]
            squares = mine * mine
            intensity = squares[:n, :n] + squares[:n, n:] + (squares[n:, :n] + squares[n:, n:])
            scaling = (meas_ref[s] * lax.rsqrt(jnp.maximum(intensity, AMP_FLOOR * AMP_FLOOR)) - 1.0) * live
            scaling = jnp.concatenate([scaling, scaling], axis=1)
            scaled.append(mine * jnp.concatenate([scaling, scaling], axis=0))
        middle = right(jnp.concatenate(scaled, axis=0), right_ref[1])
        added = [0.0] * 5
        for k, s in enumerate(numbers):
            live = jnp.where(s < cnt_ref[0, 0], 1.0, 0.0).astype(F32)
            qr, qi = cuts[k]
            rows, near, shift = starts[k]
            back = left(left_ref[0], swap_blocks(middle[2 * n * k : 2 * n * (k + 1)], n))
            br = [back[:n, :n], back[:n, n:]]
            bi = [back[n:, :n], back[n:, n:]]
            for m in range(2):
                added[m] += qr * br[m] + qi * bi[m]
                added[2 + m] += qr * bi[m] - qi * br[m]
            added[4] += live * (qr * qr + qi * qi)
            terms = (
                pr[0] * br[0] + pi[0] * bi[0] + (pr[1] * br[1] + pi[1] * bi[1]),
                pr[0] * bi[0] - pi[0] * br[0] + (pr[1] * bi[1] - pi[1] * br[1]),
            )
            for part in range(2):
                term = pltpu.roll(terms[part] * inverse, shift, 1)
                grad_ref[part, near, rows] += jnp.where(lane >= shift, term, 0.0)
                grad_ref[part, near + 1, rows] += jnp.where(lane < shift, term, 0.0)
        for ch in range(5):
            sums[ch] += added[ch]
        return carry

    lax.fori_loop(0, slots // group, some_slots, 0)
    per = n // 8
    for g in range(2 * red_ref.shape[1] * share):
        h, k = divmod(g, red_ref.shape[1] * share)
        t = h * half + k
        used = k < half and t < tiles
        value = sums[t // per, 8 * (t % per) : 8 * (t % per) + 8] if used else jnp.zeros((8, n), F32)
        red_ref[h, k // share, k % share] = value


def finish_kernel(
    nrow, ncol, n, shares,
    grad_ref, red_ref, obj_ref, probe_ref,
    got0, acc0, got1, acc1, got2, every, in_right, in_corner, in_below, rim,
    send0, recv0, send1, recv1, send2, recv2, send3, recv3, send4, recv4, send_spill, recv_spill,
):
    _, height, width = obj_ref.shape
    tiles, half, share = shares
    blocks = width // n
    nchip = ncol // 2
    r, c = place()
    chip, core = c // 2, lax.rem(c, 2)
    down = lax.rem(r + 1, nrow)
    west, east = lax.rem(c + ncol - 1, ncol), lax.rem(c + 1, ncol)
    twin = (r, c + 1 - 2 * core)
    row_peer = lambda d: (lax.rem(r + d, nrow), c)
    chip_peer = lambda d: (r, lax.rem(chip + d, nchip) * 2 + core)
    barrier = pltpu.get_barrier_semaphore()
    peers = [row_peer(d) for d in range(1, nrow)] + [chip_peer(d) for d in range(1, nchip)]
    peers += [(r, west), (r, east)]
    for peer in peers:
        pl.semaphore_signal(barrier, inc=1, device_id=peer, device_id_type=MESH)
    pl.semaphore_wait(barrier, len(peers))

    pair = remote(red_ref.at[1 - core], got0, send0.at[0], recv0.at[0], twin)
    pair.start()

    corner = remote(grad_ref.at[:, blocks, height:], in_corner, send_spill.at[0], recv_spill.at[0], (r, east))
    beside = remote(grad_ref.at[:, blocks, :height], in_right, send_spill.at[1], recv_spill.at[1], (r, east))
    below = [
        remote(
            rim if b == 0 else grad_ref.at[:, b, height:],
            in_below.at[:, b], send_spill.at[2 + b], recv_spill.at[2 + b], (down, c),
        )
        for b in range(blocks)
    ]

    @pl.when(c < ncol - 1)
    def _():
        corner.start()
        beside.start()

    pair.wait_recv()
    acc0[...] = red_ref[core] + got0[...]
    first = []
    for d in range(1, nrow):
        peer = row_peer(d)
        first.append(remote(acc0.at[peer[0]], got1.at[r], send1.at[d], recv1.at[d], peer))
        first[-1].start()

    for b in range(blocks):
        obj_ref[:, :, b * n : (b + 1) * n] = grad_ref[:, b, :height]
    rim[...] = grad_ref[:, 0, height:]

    for one in first:
        one.wait_recv()
    total = acc0[r]
    for d in range(1, nrow):
        total = total + got1[lax.rem(r + nrow - d, nrow)]
    acc1[...] = total

    second = []
    for d in range(1, nchip):
        second.append(remote(acc1, got2.at[chip], send2.at[d], recv2.at[d], chip_peer(d)))
        second[-1].start()
    got2[chip] = total

    @pl.when(c > 0)
    def _():
        corner.wait_recv()
        rim[...] += in_corner[...]

    @pl.when(r < nrow - 1)
    def _():
        for one in below:
            one.start()

    for one in second:
        one.wait_recv()
    total = got2[0]
    for k in range(1, nchip):
        total = total + got2[k]
    every[core, r] = total

    third = []
    for d in range(1, nrow):
        piece = every.at[core, r]
        third.append(remote(piece, piece, send3.at[d], recv3.at[d], row_peer(d)))
        third[-1].start()

    @pl.when(c > 0)
    def _():
        beside.wait_recv()
        obj_ref[:, :, :n] += in_right[...]

    for one in third:
        one.wait_recv()
    fourth = remote(every.at[core], every.at[core], send4.at[0], recv4.at[0], twin)
    fourth.start()

    @pl.when(r > 0)
    def _():
        for b, one in enumerate(below):
            one.wait_recv()
            obj_ref[:, :n, b * n : (b + 1) * n] += in_below[:, b]

    fourth.wait_recv()

    per = n // 8

    def tile(g):
        k = g % half
        return every[g // half, k // share, k % share]

    for i in range(per):
        factor = lax.rsqrt(tile(4 * per + i) + 1.0)
        for ch in range(4):
            probe_ref[ch // 2, ch % 2, 8 * i : 8 * i + 8] = tile(ch * per + i) * factor

    for one in [pair] + first + second + third + [fourth]:
        one.wait_send()

    @pl.when(c < ncol - 1)
    def _():
        corner.wait_send()
        beside.wait_send()

    @pl.when(r < nrow - 1)
    def _():
        for one in below:
            one.wait_send()


def per_device(nrow, ncol, tables, object_field, probe_modes, measured, positions, counts):
    n = probe_modes.shape[-1]
    _, height, width = object_field.shape
    blocks, slots = width // n, measured.shape[2]
    shares = tiles, half, share = tiling(nrow, n)
    group = 4 if slots % 4 == 0 else 1
    params = functools.partial(pltpu.CompilerParams, vmem_limit_bytes=LIMIT)
    dma = pltpu.SemaphoreType.DMA
    extended = pl.pallas_call(
        functools.partial(halo_kernel, nrow, ncol, n),
        out_shape=jax.ShapeDtypeStruct((2, blocks + 1, height + n, n), F32),
        in_specs=[pl.BlockSpec(memory_space=pl.ANY)],
        out_specs=VMEM,
        scratch_shapes=[dma((blocks + 2,)), dma((blocks + 2,)), dma((blocks,))],
        compiler_params=params(collective_id=0, has_side_effects=True),
    )(object_field)
    gradient, sums = pl.pallas_call(
        functools.partial(compute_kernel, shares, group, height, width),
        out_shape=(
            jax.ShapeDtypeStruct((2, blocks + 1, height + n, n), F32),
            jax.ShapeDtypeStruct((2, nrow, share, 8, n), F32),
        ),
        in_specs=[SMEM, SMEM] + [VMEM] * 5,
        out_specs=(VMEM, VMEM),
        scratch_shapes=[pltpu.VMEM((5, n, n), F32)],
        compiler_params=params(),
    )(positions[0, 0], counts, extended, probe_modes, measured[0, 0], *tables)
    return pl.pallas_call(
        functools.partial(finish_kernel, nrow, ncol, n, shares),
        out_shape=(
            jax.ShapeDtypeStruct((2, height, width), F32),
            jax.ShapeDtypeStruct((2, 2, n, n), F32),
        ),
        in_specs=[VMEM, VMEM],
        out_specs=(VMEM, VMEM),
        scratch_shapes=[
            pltpu.VMEM((nrow, share, 8, n), F32),
            pltpu.VMEM((nrow, share, 8, n), F32),
            pltpu.VMEM((nrow, share, 8, n), F32),
            pltpu.VMEM((share, 8, n), F32),
            pltpu.VMEM((ncol // 2, share, 8, n), F32),
            pltpu.VMEM((2, nrow, share, 8, n), F32),
            pltpu.VMEM((2, height, n), F32),
            pltpu.VMEM((2, n, n), F32),
            pltpu.VMEM((2, blocks, n, n), F32),
            pltpu.VMEM((2, n, n), F32),
        ]
        + [dma((k,)) for k in (1, 1, nrow, nrow, ncol // 2, ncol // 2, nrow, nrow, 1, 1, 2 + blocks, 2 + blocks)],
        compiler_params=params(collective_id=1, has_side_effects=True),
    )(gradient, sums)


def solution(mesh):
    nrow, ncol = mesh.shape["row"], mesh.shape["col"]
    in_specs = (
        P(None, "row", "col"),
        P(),
        P("row", "col", None, None, None),
        P("row", "col", None, None),
        P("row", "col"),
    )
    out_specs = (P(None, "row", "col"), P())

    def run(object_field, probe_modes, measured, positions, counts):
        tables = [jnp.asarray(t) for t in fourier_tables(probe_modes.shape[-1])]
        return jax.shard_map(
            functools.partial(per_device, nrow, ncol, tables),
            mesh=mesh, in_specs=in_specs, out_specs=out_specs, check_vma=False,
        )(object_field, probe_modes, measured, positions, counts)

    return run
```

```python
import functools
import math

import jax
import jax.numpy as jnp
import ml_dtypes
import numpy as np
from jax import lax
from jax.experimental import pallas as pl
from jax.experimental.pallas import tpu as pltpu
from jax.sharding import PartitionSpec as P

AMP_FLOOR = 0.25
F32 = jnp.float32
MESH = pl.DeviceIdType.MESH
VMEM = pl.BlockSpec(memory_space=pltpu.VMEM)
SMEM = pl.BlockSpec(memory_space=pltpu.SMEM)
HBM = pl.BlockSpec(memory_space=pltpu.HBM)
LIMIT = 48 * 1024 * 1024


def fourier_tables(n):
    index = np.arange(n)
    angle = (index[:, None] * index[None, :] % n) * (2.0 * math.pi / n)
    c = np.cos(angle) / math.sqrt(n)
    s = np.sin(angle) / math.sqrt(n)
    a = np.block([[c, -s], [s, c]]).astype(np.float32)
    on_left, on_right = [], []
    for w in (a, a.T):
        hi = w.astype(ml_dtypes.bfloat16)
        lo = (w - hi.astype(np.float32)).astype(ml_dtypes.bfloat16)
        on_left.append(np.concatenate([hi, lo, hi], axis=1))
        on_right.append(np.concatenate([hi, lo, hi], axis=0))
    return np.stack(on_left), np.stack(on_right)


def split(x):
    hi = x.astype(jnp.bfloat16)
    return hi, (x - hi.astype(F32)).astype(jnp.bfloat16)


def left(table, x):
    hi, lo = split(x)
    return jnp.dot(table, jnp.concatenate([hi, hi, lo], axis=0), preferred_element_type=F32)


def right(x, table):
    hi, lo = split(x)
    return jnp.dot(jnp.concatenate([hi, hi, lo], axis=1), table, preferred_element_type=F32)


def swap_blocks(x, n):
    return jnp.concatenate(
        [
            jnp.concatenate([x[:n, :n], x[n:, :n]], axis=1),
            jnp.concatenate([x[:n, n:], x[n:, n:]], axis=1),
        ],
        axis=0,
    )


def tiling(nrow, n):
    tiles = 5 * (n // 8)
    half = -(-tiles // 2)
    return tiles, half, -(-half // nrow)


def place():
    return lax.axis_index("row"), lax.axis_index("col")


def remote(src, dst, send_sem, recv_sem, peer):
    return pltpu.make_async_remote_copy(
        src_ref=src, dst_ref=dst, send_sem=send_sem, recv_sem=recv_sem, device_id=peer, device_id_type=MESH
    )


def halo_kernel(nrow, ncol, n, obj_ref, ext_ref, send_sem, recv_sem, own_sem):
    _, height, width = obj_ref.shape
    blocks = width // n
    r, c = place()
    up, down = lax.rem(r + nrow - 1, nrow), lax.rem(r + 1, nrow)
    west, east = lax.rem(c + ncol - 1, ncol), lax.rem(c + 1, ncol)
    own = [
        pltpu.make_async_copy(obj_ref.at[:, :, b * n : (b + 1) * n], ext_ref.at[:, b, :height], own_sem.at[b])
        for b in range(blocks)
    ]
    barrier = pltpu.get_barrier_semaphore()
    for peer in ((up, c), (down, c), (r, west), (r, east)):
        pl.semaphore_signal(barrier, inc=1, device_id=peer, device_id_type=MESH)
    pl.semaphore_wait(barrier, 4)

    below = []
    for b in range(blocks):
        source = obj_ref.at[:, :n, b * n : (b + 1) * n]
        below.append(remote(source, ext_ref.at[:, b, height:], send_sem.at[b], recv_sem.at[b], (up, c)))
    right_halo = ext_ref.at[:, blocks, :height]
    corner_halo = ext_ref.at[:, blocks, height:]
    beside = remote(
        obj_ref.at[:, :, :n], right_halo, send_sem.at[blocks], recv_sem.at[blocks], (r, west)
    )
    corner = remote(
        ext_ref.at[:, 0, height:], corner_halo, send_sem.at[blocks + 1], recv_sem.at[blocks + 1], (r, west)
    )
    has_below, has_right = r < nrow - 1, c < ncol - 1

    @pl.when(r > 0)
    def _():
        below[0].start()

    @pl.when(c > 0)
    def _():
        beside.start()

    for one in own:
        one.start()

    @pl.when(jnp.logical_not(has_below))
    def _():
        ext_ref[:, :, height:] = jnp.zeros((2, blocks + 1, n, n), F32)

    @pl.when(jnp.logical_not(has_right))
    def _():
        ext_ref[:, blocks, :] = jnp.zeros((2, height + n, n), F32)

    @pl.when(r > 0)
    def _():
        below[0].wait_send()
        for one in below[1:]:
            one.start()

    @pl.when(has_below)
    def _():
        below[0].wait_recv()

        @pl.when(c > 0)
        def _():
            corner.start()

        for one in below[1:]:
            one.wait_recv()

    for one in own:
        one.wait()

    @pl.when(has_right)
    def _():
        beside.wait_recv()

        @pl.when(has_below)
        def _():
            corner.wait_recv()

    @pl.when(r > 0)
    def _():
        for one in below[1:]:
            one.wait_send()

    @pl.when(c > 0)
    def _():
        beside.wait_send()

        @pl.when(has_below)
        def _():
            corner.wait_send()


def compute_kernel(
    shares, group, height, width,
    pos_ref, cnt_ref, ext_ref, probe_ref, meas_ref, left_ref, right_ref, grad_ref, red_ref, sums,
):
    n = probe_ref.shape[-1]
    slots = meas_ref.shape[0]
    tiles, half, share = shares
    blocks = width // n
    pr = [probe_ref[0, 0], probe_ref[0, 1]]
    pi = [probe_ref[1, 0], probe_ref[1, 1]]
    power = pr[0] * pr[0] + pi[0] * pi[0] + (pr[1] * pr[1] + pi[1] * pi[1])
    inverse = 1.0 / (jnp.max(power, keepdims=True) + 1e-06)
    lane = lax.broadcasted_iota(jnp.int32, (n, n), 1)
    grad_ref[...] = jnp.zeros(grad_ref.shape, F32)
    grad_ref[:, :blocks, :height] = ext_ref[:, :blocks, :height]
    sums[...] = jnp.zeros(sums.shape, F32)

    def some_slots(first, carry):
        pr = [probe_ref[0, 0], probe_ref[0, 1]]
        pi = [probe_ref[1, 0], probe_ref[1, 1]]
        numbers = [first * group + k for k in range(group)]
        starts, cuts, lefts = [], [], []
        for s in numbers:
            row, col = pos_ref[0, s], pos_ref[1, s]
            near = col // n
            shift = lax.rem(col, n)
            back_shift = lax.rem(n - shift, n)
            rows = pl.ds(row, n)
            starts.append((rows, near, shift))
            patch = []
            for part in range(2):
                a = pltpu.roll(ext_ref[part, near, rows], back_shift, 1)
                b = pltpu.roll(ext_ref[part, near + 1, rows], back_shift, 1)
                patch.append(jnp.where(lane < n - shift, a, b))
            cuts.append(patch)
            qr, qi = patch
            waves = jnp.concatenate(
                [
                    jnp.concatenate([pr[m] * qr - pi[m] * qi for m in range(2)], axis=1),
                    jnp.concatenate([pr[m] * qi + pi[m] * qr for m in range(2)], axis=1),
                ],
                axis=0,
            )
            lefts.append(swap_blocks(left(left_ref[1], waves), n))
        far = right(jnp.concatenate(lefts, axis=0), right_ref[0])
        scaled = []
        for k, s in enumerate(numbers):
            live = jnp.where(s < cnt_ref[0, 0], 1.0, 0.0).astype(F32)
            mine = far[2 * n * k : 2 * n * (k + 1)]
            squares = mine * mine
            intensity = squares[:n, :n] + squares[:n, n:] + (squares[n:, :n] + squares[n:, n:])
            scaling = (meas_ref[s] * lax.rsqrt(jnp.maximum(intensity, AMP_FLOOR * AMP_FLOOR)) - 1.0) * live
            scaling = jnp.concatenate([scaling, scaling], axis=1)
            scaled.append(mine * jnp.concatenate([scaling, scaling], axis=0))
        middle = right(jnp.concatenate(scaled, axis=0), right_ref[1])
        added = [0.0] * 5
        for k, s in enumerate(numbers):
            live = jnp.where(s < cnt_ref[0, 0], 1.0, 0.0).astype(F32)
            qr, qi = cuts[k]
            rows, near, shift = starts[k]
            back = left(left_ref[0], swap_blocks(middle[2 * n * k : 2 * n * (k + 1)], n))
            br = [back[:n, :n], back[:n, n:]]
            bi = [back[n:, :n], back[n:, n:]]
            for m in range(2):
                added[m] += qr * br[m] + qi * bi[m]
                added[2 + m] += qr * bi[m] - qi * br[m]
            added[4] += live * (qr * qr + qi * qi)
            terms = (
                pr[0] * br[0] + pi[0] * bi[0] + (pr[1] * br[1] + pi[1] * bi[1]),
                pr[0] * bi[0] - pi[0] * br[0] + (pr[1] * bi[1] - pi[1] * br[1]),
            )
            for part in range(2):
                term = pltpu.roll(terms[part] * inverse, shift, 1)
                grad_ref[part, near, rows] += jnp.where(lane >= shift, term, 0.0)
                grad_ref[part, near + 1, rows] += jnp.where(lane < shift, term, 0.0)
        for ch in range(5):
            sums[ch] += added[ch]
        return carry

    lax.fori_loop(0, slots // group, some_slots, 0)
    per = n // 8
    for g in range(2 * red_ref.shape[1] * share):
        h, k = divmod(g, red_ref.shape[1] * share)
        t = h * half + k
        used = k < half and t < tiles
        value = sums[t // per, 8 * (t % per) : 8 * (t % per) + 8] if used else jnp.zeros((8, n), F32)
        red_ref[h, k // share, k % share] = value


def finish_kernel(
    nrow, ncol, n, shares,
    grad_ref, red_ref, obj_ref, every,
    got0, acc0, got1, acc1, got2, in_right, in_corner, in_below, rim,
    send0, recv0, send1, recv1, send2, recv2, send3, recv3, send4, recv4, send_spill, recv_spill,
):
    _, height, width = obj_ref.shape
    tiles, half, share = shares
    blocks = width // n
    nchip = ncol // 2
    r, c = place()
    chip, core = c // 2, lax.rem(c, 2)
    down = lax.rem(r + 1, nrow)
    west, east = lax.rem(c + ncol - 1, ncol), lax.rem(c + 1, ncol)
    twin = (r, c + 1 - 2 * core)
    row_peer = lambda d: (lax.rem(r + d, nrow), c)
    chip_peer = lambda d: (r, lax.rem(chip + d, nchip) * 2 + core)
    barrier = pltpu.get_barrier_semaphore()
    peers = [row_peer(d) for d in range(1, nrow)] + [chip_peer(d) for d in range(1, nchip)]
    peers += [(r, west), (r, east)]
    for peer in peers:
        pl.semaphore_signal(barrier, inc=1, device_id=peer, device_id_type=MESH)
    pl.semaphore_wait(barrier, len(peers))

    pair = remote(red_ref.at[1 - core], got0, send0.at[0], recv0.at[0], twin)
    pair.start()

    corner = remote(grad_ref.at[:, blocks, height:], in_corner, send_spill.at[0], recv_spill.at[0], (r, east))
    beside = remote(grad_ref.at[:, blocks, :height], in_right, send_spill.at[1], recv_spill.at[1], (r, east))
    below = [
        remote(
            rim if b == 0 else grad_ref.at[:, b, height:],
            in_below.at[:, b], send_spill.at[2 + b], recv_spill.at[2 + b], (down, c),
        )
        for b in range(blocks)
    ]

    @pl.when(c < ncol - 1)
    def _():
        corner.start()
        beside.start()

    pair.wait_recv()
    acc0[...] = red_ref[core] + got0[...]
    first = []
    for d in range(1, nrow):
        peer = row_peer(d)
        first.append(remote(acc0.at[peer[0]], got1.at[r], send1.at[d], recv1.at[d], peer))
        first[-1].start()

    for b in range(blocks):
        obj_ref[:, :, b * n : (b + 1) * n] = grad_ref[:, b, :height]
    rim[...] = grad_ref[:, 0, height:]

    for one in first:
        one.wait_recv()

    @pl.when(r < nrow - 1)
    def _():
        for one in below[1:]:
            one.start()

    total = acc0[r]
    for d in range(1, nrow):
        total = total + got1[lax.rem(r + nrow - d, nrow)]
    acc1[...] = total

    second = []
    for d in range(1, nchip):
        second.append(remote(acc1, got2.at[chip], send2.at[d], recv2.at[d], chip_peer(d)))
        second[-1].start()
    got2[chip] = total

    @pl.when(c > 0)
    def _():
        corner.wait_recv()
        rim[...] += in_corner[...]

    @pl.when(r < nrow - 1)
    def _():
        below[0].start()

    for one in second:
        one.wait_recv()
    total = got2[0]
    for k in range(1, nchip):
        total = total + got2[k]
    every[core, r] = total

    third = []
    for d in range(1, nrow):
        piece = every.at[core, r]
        third.append(remote(piece, piece, send3.at[d], recv3.at[d], row_peer(d)))
        third[-1].start()

    @pl.when(c > 0)
    def _():
        beside.wait_recv()
        obj_ref[:, :, :n] += in_right[...]

    for one in third:
        one.wait_recv()
    fourth = remote(every.at[core], every.at[core], send4.at[0], recv4.at[0], twin)
    fourth.start()

    @pl.when(r > 0)
    def _():
        for b, one in enumerate(below):
            one.wait_recv()
            obj_ref[:, :n, b * n : (b + 1) * n] += in_below[:, b]

    fourth.wait_recv()

    for one in [pair] + first + second + third + [fourth]:
        one.wait_send()

    @pl.when(c < ncol - 1)
    def _():
        corner.wait_send()
        beside.wait_send()

    @pl.when(r < nrow - 1)
    def _():
        for one in below:
            one.wait_send()


def result_kernel(shares, obj_ref, every, object_out, probe_out, probe, sems):
    tiles, half, share = shares
    n = probe.shape[-1]
    per = n // 8
    objects = pltpu.make_async_copy(obj_ref, object_out, sems.at[0])
    objects.start()

    def tile(g):
        k = g % half
        return every[g // half, k // share, k % share]

    for i in range(per):
        factor = lax.rsqrt(tile(4 * per + i) + 1.0)
        for ch in range(4):
            probe[ch // 2, ch % 2, 8 * i : 8 * i + 8] = tile(ch * per + i) * factor
    steps = pltpu.make_async_copy(probe, probe_out, sems.at[1])
    steps.start()
    objects.wait()
    steps.wait()


def per_device(nrow, ncol, tables, object_field, probe_modes, measured, positions, counts):
    n = probe_modes.shape[-1]
    _, height, width = object_field.shape
    blocks, slots = width // n, measured.shape[2]
    shares = tiles, half, share = tiling(nrow, n)
    group = 4 if slots % 4 == 0 else 1
    params = functools.partial(pltpu.CompilerParams, vmem_limit_bytes=LIMIT)
    dma = pltpu.SemaphoreType.DMA
    extended = pl.pallas_call(
        functools.partial(halo_kernel, nrow, ncol, n),
        out_shape=jax.ShapeDtypeStruct((2, blocks + 1, height + n, n), F32),
        in_specs=[HBM],
        out_specs=VMEM,
        scratch_shapes=[dma((blocks + 2,)), dma((blocks + 2,)), dma((blocks,))],
        compiler_params=params(collective_id=0, has_side_effects=True),
    )(object_field)
    gradient, sums = pl.pallas_call(
        functools.partial(compute_kernel, shares, group, height, width),
        out_shape=(
            jax.ShapeDtypeStruct((2, blocks + 1, height + n, n), F32),
            jax.ShapeDtypeStruct((2, nrow, share, 8, n), F32),
        ),
        in_specs=[SMEM, SMEM] + [VMEM] * 5,
        out_specs=(VMEM, VMEM),
        scratch_shapes=[pltpu.VMEM((5, n, n), F32)],
        compiler_params=params(),
    )(positions[0, 0], counts, extended, probe_modes, measured[0, 0], *tables)
    object_new, total = pl.pallas_call(
        functools.partial(finish_kernel, nrow, ncol, n, shares),
        out_shape=(
            jax.ShapeDtypeStruct((2, height, width), F32),
            jax.ShapeDtypeStruct((2, nrow, share, 8, n), F32),
        ),
        in_specs=[VMEM, VMEM],
        out_specs=(VMEM, VMEM),
        scratch_shapes=[
            pltpu.VMEM((nrow, share, 8, n), F32),
            pltpu.VMEM((nrow, share, 8, n), F32),
            pltpu.VMEM((nrow, share, 8, n), F32),
            pltpu.VMEM((share, 8, n), F32),
            pltpu.VMEM((ncol // 2, share, 8, n), F32),
            pltpu.VMEM((2, height, n), F32),
            pltpu.VMEM((2, n, n), F32),
            pltpu.VMEM((2, blocks, n, n), F32),
            pltpu.VMEM((2, n, n), F32),
        ]
        + [dma((k,)) for k in (1, 1, nrow, nrow, ncol // 2, ncol // 2, nrow, nrow, 1, 1, 2 + blocks, 2 + blocks)],
        compiler_params=params(collective_id=1, has_side_effects=True),
    )(gradient, sums)
    return pl.pallas_call(
        functools.partial(result_kernel, shares),
        out_shape=(
            jax.ShapeDtypeStruct((2, height, width), F32),
            jax.ShapeDtypeStruct((2, 2, n, n), F32),
        ),
        in_specs=[VMEM, VMEM],
        out_specs=(HBM, HBM),
        scratch_shapes=[pltpu.VMEM((2, 2, n, n), F32), dma((2,))],
        compiler_params=params(),
    )(object_new, total)


def solution(mesh):
    nrow, ncol = mesh.shape["row"], mesh.shape["col"]
    in_specs = (
        P(None, "row", "col"),
        P(),
        P("row", "col", None, None, None),
        P("row", "col", None, None),
        P("row", "col"),
    )
    out_specs = (P(None, "row", "col"), P())

    def run(object_field, probe_modes, measured, positions, counts):
        tables = [jnp.asarray(t) for t in fourier_tables(probe_modes.shape[-1])]
        return jax.shard_map(
            functools.partial(per_device, nrow, ncol, tables),
            mesh=mesh, in_specs=in_specs, out_specs=out_specs, check_vma=False,
        )(object_field, probe_modes, measured, positions, counts)

    return run
```

```python
import functools
import math

import jax
import jax.numpy as jnp
import ml_dtypes
import numpy as np
from jax import lax
from jax.experimental import pallas as pl
from jax.experimental.pallas import tpu as pltpu
from jax.sharding import PartitionSpec as P

AMP_FLOOR = 0.25
F32 = jnp.float32
MESH = pl.DeviceIdType.MESH
VMEM = pl.BlockSpec(memory_space=pltpu.VMEM)
SMEM = pl.BlockSpec(memory_space=pltpu.SMEM)
HBM = pl.BlockSpec(memory_space=pltpu.HBM)
LIMIT = 48 * 1024 * 1024


def fourier_tables(n):
    index = np.arange(n)
    angle = (index[:, None] * index[None, :] % n) * (2.0 * math.pi / n)
    c = np.cos(angle) / math.sqrt(n)
    s = np.sin(angle) / math.sqrt(n)
    a = np.block([[c, -s], [s, c]]).astype(np.float32)
    on_left, on_right = [], []
    for w in (a, a.T):
        hi = w.astype(ml_dtypes.bfloat16)
        lo = (w - hi.astype(np.float32)).astype(ml_dtypes.bfloat16)
        on_left.append(np.concatenate([hi, lo, hi], axis=1))
        on_right.append(np.concatenate([hi, lo, hi], axis=0))
    return np.stack(on_left), np.stack(on_right)


def split(x):
    hi = x.astype(jnp.bfloat16)
    return hi, (x - hi.astype(F32)).astype(jnp.bfloat16)


def left(table, x):
    hi, lo = split(x)
    return jnp.dot(table, jnp.concatenate([hi, hi, lo], axis=0), preferred_element_type=F32)


def right(x, table):
    hi, lo = split(x)
    return jnp.dot(jnp.concatenate([hi, hi, lo], axis=1), table, preferred_element_type=F32)


def swap_blocks(x, n):
    return jnp.concatenate(
        [
            jnp.concatenate([x[:n, :n], x[n:, :n]], axis=1),
            jnp.concatenate([x[:n, n:], x[n:, n:]], axis=1),
        ],
        axis=0,
    )


def tiling(nrow, n):
    tiles = 5 * (n // 8)
    half = -(-tiles // 2)
    return tiles, half, -(-half // nrow)


def place():
    return lax.axis_index("row"), lax.axis_index("col")


def remote(src, dst, send_sem, recv_sem, peer):
    return pltpu.make_async_remote_copy(
        src_ref=src, dst_ref=dst, send_sem=send_sem, recv_sem=recv_sem, device_id=peer, device_id_type=MESH
    )


def halo_kernel(nrow, ncol, n, obj_ref, ext_ref, send_sem, recv_sem, own_sem):
    _, height, width = obj_ref.shape
    blocks = width // n
    r, c = place()
    up, down = lax.rem(r + nrow - 1, nrow), lax.rem(r + 1, nrow)
    west, east = lax.rem(c + ncol - 1, ncol), lax.rem(c + 1, ncol)
    own = [
        pltpu.make_async_copy(obj_ref.at[:, :, b * n : (b + 1) * n], ext_ref.at[:, b, :height], own_sem.at[b])
        for b in range(blocks)
    ]
    barrier = pltpu.get_barrier_semaphore()
    for peer in ((up, c), (down, c), (r, west), (r, east)):
        pl.semaphore_signal(barrier, inc=1, device_id=peer, device_id_type=MESH)
    pl.semaphore_wait(barrier, 4)

    def piece(index, src, dst, peer):
        return remote(src, dst, send_sem.at[index], recv_sem.at[index], peer)

    below = [
        [
            piece(
                2 * b + part,
                obj_ref.at[part, :n, b * n : (b + 1) * n],
                ext_ref.at[part, b, height:],
                (up, c),
            )
            for part in range(2)
        ]
        for b in range(blocks)
    ]
    later = [one for b in range(1, blocks) for one in below[b]]
    sooner, later = later[: len(later) // 2], later[len(later) // 2 :]
    beside = piece(2 * blocks, obj_ref.at[:, :, :n], ext_ref.at[:, blocks, :height], (r, west))
    corner = [
        piece(
            2 * blocks + 1 + part,
            ext_ref.at[part, 0, height:],
            ext_ref.at[part, blocks, height:],
            (r, west),
        )
        for part in range(2)
    ]
    has_below, has_right = r < nrow - 1, c < ncol - 1

    @pl.when(r > 0)
    def _():
        for one in below[0]:
            one.start()

    @pl.when(c > 0)
    def _():
        beside.start()

    for one in own:
        one.start()

    @pl.when(jnp.logical_not(has_below))
    def _():
        ext_ref[:, :, height:] = jnp.zeros((2, blocks + 1, n, n), F32)

    @pl.when(jnp.logical_not(has_right))
    def _():
        ext_ref[:, blocks, :] = jnp.zeros((2, height + n, n), F32)

    @pl.when(r > 0)
    def _():
        for one in below[0]:
            one.wait_send()
        for one in sooner:
            one.start()

    @pl.when(has_below)
    def _():
        for part in range(2):
            below[0][part].wait_recv()

            @pl.when(c > 0)
            def _():
                corner[part].start()

    @pl.when(r > 0)
    def _():
        for one in later:
            one.start()

    @pl.when(has_below)
    def _():
        for one in sooner + later:
            one.wait_recv()

    for one in own:
        one.wait()

    @pl.when(has_right)
    def _():
        beside.wait_recv()

        @pl.when(has_below)
        def _():
            for one in corner:
                one.wait_recv()

    @pl.when(r > 0)
    def _():
        for one in sooner + later:
            one.wait_send()

    @pl.when(c > 0)
    def _():
        beside.wait_send()

        @pl.when(has_below)
        def _():
            for one in corner:
                one.wait_send()


def compute_kernel(
    shares, group, height, width,
    pos_ref, cnt_ref, ext_ref, probe_ref, meas_ref, left_ref, right_ref, grad_ref, red_ref, sums,
):
    n = probe_ref.shape[-1]
    slots = meas_ref.shape[0]
    tiles, half, share = shares
    blocks = width // n
    pr = [probe_ref[0, 0], probe_ref[0, 1]]
    pi = [probe_ref[1, 0], probe_ref[1, 1]]
    power = pr[0] * pr[0] + pi[0] * pi[0] + (pr[1] * pr[1] + pi[1] * pi[1])
    inverse = 1.0 / (jnp.max(power, keepdims=True) + 1e-06)
    lane = lax.broadcasted_iota(jnp.int32, (n, n), 1)
    grad_ref[...] = jnp.zeros(grad_ref.shape, F32)
    grad_ref[:, :blocks, :height] = ext_ref[:, :blocks, :height]
    sums[...] = jnp.zeros(sums.shape, F32)

    def some_slots(first, carry):
        pr = [probe_ref[0, 0], probe_ref[0, 1]]
        pi = [probe_ref[1, 0], probe_ref[1, 1]]
        numbers = [first * group + k for k in range(group)]
        starts, cuts, lefts = [], [], []
        for s in numbers:
            row, col = pos_ref[0, s], pos_ref[1, s]
            near = col // n
            shift = lax.rem(col, n)
            back_shift = lax.rem(n - shift, n)
            rows = pl.ds(row, n)
            starts.append((rows, near, shift))
            patch = []
            for part in range(2):
                a = pltpu.roll(ext_ref[part, near, rows], back_shift, 1)
                b = pltpu.roll(ext_ref[part, near + 1, rows], back_shift, 1)
                patch.append(jnp.where(lane < n - shift, a, b))
            cuts.append(patch)
            qr, qi = patch
            waves = jnp.concatenate(
                [
                    jnp.concatenate([pr[m] * qr - pi[m] * qi for m in range(2)], axis=1),
                    jnp.concatenate([pr[m] * qi + pi[m] * qr for m in range(2)], axis=1),
                ],
                axis=0,
            )
            lefts.append(swap_blocks(left(left_ref[1], waves), n))
        far = right(jnp.concatenate(lefts, axis=0), right_ref[0])
        scaled = []
        for k, s in enumerate(numbers):
            live = jnp.where(s < cnt_ref[0, 0], 1.0, 0.0).astype(F32)
            mine = far[2 * n * k : 2 * n * (k + 1)]
            squares = mine * mine
            intensity = squares[:n, :n] + squares[:n, n:] + (squares[n:, :n] + squares[n:, n:])
            scaling = (meas_ref[s] * lax.rsqrt(jnp.maximum(intensity, AMP_FLOOR * AMP_FLOOR)) - 1.0) * live
            scaling = jnp.concatenate([scaling, scaling], axis=1)
            scaled.append(mine * jnp.concatenate([scaling, scaling], axis=0))
        middle = right(jnp.concatenate(scaled, axis=0), right_ref[1])
        added = [0.0] * 5
        for k, s in enumerate(numbers):
            live = jnp.where(s < cnt_ref[0, 0], 1.0, 0.0).astype(F32)
            qr, qi = cuts[k]
            rows, near, shift = starts[k]
            back = left(left_ref[0], swap_blocks(middle[2 * n * k : 2 * n * (k + 1)], n))
            br = [back[:n, :n], back[:n, n:]]
            bi = [back[n:, :n], back[n:, n:]]
            for m in range(2):
                added[m] += qr * br[m] + qi * bi[m]
                added[2 + m] += qr * bi[m] - qi * br[m]
            added[4] += live * (qr * qr + qi * qi)
            terms = (
                pr[0] * br[0] + pi[0] * bi[0] + (pr[1] * br[1] + pi[1] * bi[1]),
                pr[0] * bi[0] - pi[0] * br[0] + (pr[1] * bi[1] - pi[1] * br[1]),
            )
            for part in range(2):
                term = pltpu.roll(terms[part] * inverse, shift, 1)
                grad_ref[part, near, rows] += jnp.where(lane >= shift, term, 0.0)
                grad_ref[part, near + 1, rows] += jnp.where(lane < shift, term, 0.0)
        for ch in range(5):
            sums[ch] += added[ch]
        return carry

    lax.fori_loop(0, slots // group, some_slots, 0)
    per = n // 8
    for g in range(2 * red_ref.shape[1] * share):
        h, k = divmod(g, red_ref.shape[1] * share)
        t = h * half + k
        used = k < half and t < tiles
        value = sums[t // per, 8 * (t % per) : 8 * (t % per) + 8] if used else jnp.zeros((8, n), F32)
        red_ref[h, k // share, k % share] = value


def finish_kernel(
    nrow, ncol, n, shares,
    grad_ref, red_ref, obj_ref, every,
    got0, acc0, got1, acc1, got2, in_right, in_corner, in_below, rim,
    send0, recv0, send1, recv1, send2, recv2, send3, recv3, send4, recv4, send_spill, recv_spill,
):
    _, height, width = obj_ref.shape
    tiles, half, share = shares
    blocks = width // n
    nchip = ncol // 2
    r, c = place()
    chip, core = c // 2, lax.rem(c, 2)
    down = lax.rem(r + 1, nrow)
    west, east = lax.rem(c + ncol - 1, ncol), lax.rem(c + 1, ncol)
    twin = (r, c + 1 - 2 * core)
    row_peer = lambda d: (lax.rem(r + d, nrow), c)
    chip_peer = lambda d: (r, lax.rem(chip + d, nchip) * 2 + core)
    barrier = pltpu.get_barrier_semaphore()
    peers = [row_peer(d) for d in range(1, nrow)] + [chip_peer(d) for d in range(1, nchip)]
    peers += [(r, west), (r, east)]
    for peer in peers:
        pl.semaphore_signal(barrier, inc=1, device_id=peer, device_id_type=MESH)
    pl.semaphore_wait(barrier, len(peers))

    pair = remote(red_ref.at[1 - core], got0, send0.at[0], recv0.at[0], twin)
    pair.start()

    corner = remote(grad_ref.at[:, blocks, height:], in_corner, send_spill.at[0], recv_spill.at[0], (r, east))
    beside = [
        remote(
            grad_ref.at[part, blocks, :height], in_right.at[part],
            send_spill.at[1 + part], recv_spill.at[1 + part], (r, east),
        )
        for part in range(2)
    ]
    below = [
        remote(
            rim if b == 0 else grad_ref.at[:, b, height:],
            in_below.at[:, b], send_spill.at[3 + b], recv_spill.at[3 + b], (down, c),
        )
        for b in range(blocks)
    ]

    @pl.when(c < ncol - 1)
    def _():
        corner.start()
        beside[0].start()

    pair.wait_recv()
    acc0[...] = red_ref[core] + got0[...]
    first = []
    for d in range(1, nrow):
        peer = row_peer(d)
        first.append(remote(acc0.at[peer[0]], got1.at[r], send1.at[d], recv1.at[d], peer))
        first[-1].start()

    for b in range(blocks):
        obj_ref[:, :, b * n : (b + 1) * n] = grad_ref[:, b, :height]
    rim[...] = grad_ref[:, 0, height:]

    for one in first:
        one.wait_recv()

    @pl.when(r < nrow - 1)
    def _():
        for one in below[1:]:
            one.start()

    total = acc0[r]
    for d in range(1, nrow):
        total = total + got1[lax.rem(r + nrow - d, nrow)]
    acc1[...] = total

    second = []
    for d in range(1, nchip):
        second.append(remote(acc1, got2.at[chip], send2.at[d], recv2.at[d], chip_peer(d)))
        second[-1].start()
    got2[chip] = total

    @pl.when(c > 0)
    def _():
        corner.wait_recv()
        rim[...] += in_corner[...]

    @pl.when(r < nrow - 1)
    def _():
        below[0].start()

    for one in second:
        one.wait_recv()

    @pl.when(c < ncol - 1)
    def _():
        beside[1].start()

    total = got2[0]
    for k in range(1, nchip):
        total = total + got2[k]
    every[core, r] = total

    third = []
    for d in range(1, nrow):
        piece = every.at[core, r]
        third.append(remote(piece, piece, send3.at[d], recv3.at[d], row_peer(d)))
        third[-1].start()

    @pl.when(c > 0)
    def _():
        beside[0].wait_recv()
        obj_ref[0, :, :n] += in_right[0]

    for one in third:
        one.wait_recv()
    fourth = remote(every.at[core], every.at[core], send4.at[0], recv4.at[0], twin)
    fourth.start()

    @pl.when(r > 0)
    def _():
        for b, one in enumerate(below):
            one.wait_recv()
            obj_ref[:, :n, b * n : (b + 1) * n] += in_below[:, b]

    @pl.when(c > 0)
    def _():
        beside[1].wait_recv()
        obj_ref[1, :, :n] += in_right[1]

    fourth.wait_recv()

    for one in [pair] + first + second + third + [fourth]:
        one.wait_send()

    @pl.when(c < ncol - 1)
    def _():
        corner.wait_send()
        beside[0].wait_send()
        beside[1].wait_send()

    @pl.when(r < nrow - 1)
    def _():
        for one in below:
            one.wait_send()


def result_kernel(shares, obj_ref, every, object_out, probe_out, probe, sems):
    tiles, half, share = shares
    n = probe.shape[-1]
    per = n // 8
    objects = pltpu.make_async_copy(obj_ref, object_out, sems.at[0])
    objects.start()

    def tile(g):
        k = g % half
        return every[g // half, k // share, k % share]

    for i in range(per):
        factor = lax.rsqrt(tile(4 * per + i) + 1.0)
        for ch in range(4):
            probe[ch // 2, ch % 2, 8 * i : 8 * i + 8] = tile(ch * per + i) * factor
    steps = pltpu.make_async_copy(probe, probe_out, sems.at[1])
    steps.start()
    objects.wait()
    steps.wait()


def per_device(nrow, ncol, tables, object_field, probe_modes, measured, positions, counts):
    n = probe_modes.shape[-1]
    _, height, width = object_field.shape
    blocks, slots = width // n, measured.shape[2]
    shares = tiles, half, share = tiling(nrow, n)
    group = 4 if slots % 4 == 0 else 1
    params = functools.partial(pltpu.CompilerParams, vmem_limit_bytes=LIMIT)
    dma = pltpu.SemaphoreType.DMA
    extended = pl.pallas_call(
        functools.partial(halo_kernel, nrow, ncol, n),
        out_shape=jax.ShapeDtypeStruct((2, blocks + 1, height + n, n), F32),
        in_specs=[HBM],
        out_specs=VMEM,
        scratch_shapes=[dma((2 * blocks + 3,)), dma((2 * blocks + 3,)), dma((blocks,))],
        compiler_params=pltpu.CompilerParams(
            vmem_limit_bytes=60 * 1024 * 1024, collective_id=0, has_side_effects=True
        ),
    )(object_field)
    gradient, sums = pl.pallas_call(
        functools.partial(compute_kernel, shares, group, height, width),
        out_shape=(
            jax.ShapeDtypeStruct((2, blocks + 1, height + n, n), F32),
            jax.ShapeDtypeStruct((2, nrow, share, 8, n), F32),
        ),
        in_specs=[SMEM, SMEM] + [VMEM] * 5,
        out_specs=(VMEM, VMEM),
        scratch_shapes=[pltpu.VMEM((5, n, n), F32)],
        compiler_params=params(),
    )(positions[0, 0], counts, extended, probe_modes, measured[0, 0], *tables)
    object_new, total = pl.pallas_call(
        functools.partial(finish_kernel, nrow, ncol, n, shares),
        out_shape=(
            jax.ShapeDtypeStruct((2, height, width), F32),
            jax.ShapeDtypeStruct((2, nrow, share, 8, n), F32),
        ),
        in_specs=[VMEM, VMEM],
        out_specs=(VMEM, VMEM),
        scratch_shapes=[
            pltpu.VMEM((nrow, share, 8, n), F32),
            pltpu.VMEM((nrow, share, 8, n), F32),
            pltpu.VMEM((nrow, share, 8, n), F32),
            pltpu.VMEM((share, 8, n), F32),
            pltpu.VMEM((ncol // 2, share, 8, n), F32),
            pltpu.VMEM((2, height, n), F32),
            pltpu.VMEM((2, n, n), F32),
            pltpu.VMEM((2, blocks, n, n), F32),
            pltpu.VMEM((2, n, n), F32),
        ]
        + [dma((k,)) for k in (1, 1, nrow, nrow, ncol // 2, ncol // 2, nrow, nrow, 1, 1, 3 + blocks, 3 + blocks)],
        compiler_params=params(collective_id=1, has_side_effects=True),
    )(gradient, sums)
    return pl.pallas_call(
        functools.partial(result_kernel, shares),
        out_shape=(
            jax.ShapeDtypeStruct((2, height, width), F32),
            jax.ShapeDtypeStruct((2, 2, n, n), F32),
        ),
        in_specs=[VMEM, VMEM],
        out_specs=(HBM, HBM),
        scratch_shapes=[pltpu.VMEM((2, 2, n, n), F32), dma((2,))],
        compiler_params=params(),
    )(object_new, total)


def solution(mesh):
    nrow, ncol = mesh.shape["row"], mesh.shape["col"]
    in_specs = (
        P(None, "row", "col"),
        P(),
        P("row", "col", None, None, None),
        P("row", "col", None, None),
        P("row", "col"),
    )
    out_specs = (P(None, "row", "col"), P())

    def run(object_field, probe_modes, measured, positions, counts):
        tables = [jnp.asarray(t) for t in fourier_tables(probe_modes.shape[-1])]
        return jax.shard_map(
            functools.partial(per_device, nrow, ncol, tables),
            mesh=mesh, in_specs=in_specs, out_specs=out_specs, check_vma=False,
        )(object_field, probe_modes, measured, positions, counts)

    return run
```

```python
import functools
import math

import jax
import jax.numpy as jnp
import ml_dtypes
import numpy as np
from jax import lax
from jax.experimental import pallas as pl
from jax.experimental.pallas import tpu as pltpu
from jax.sharding import PartitionSpec as P

AMP_FLOOR = 0.25
F32 = jnp.float32
MESH = pl.DeviceIdType.MESH
VMEM = pl.BlockSpec(memory_space=pltpu.VMEM)
SMEM = pl.BlockSpec(memory_space=pltpu.SMEM)
HBM = pl.BlockSpec(memory_space=pltpu.HBM)
LIMIT = 48 * 1024 * 1024


def fourier_tables(n):
    index = np.arange(n)
    angle = (index[:, None] * index[None, :] % n) * (2.0 * math.pi / n)
    c = np.cos(angle) / math.sqrt(n)
    s = np.sin(angle) / math.sqrt(n)
    a = np.block([[c, -s], [s, c]]).astype(np.float32)
    on_left, on_right = [], []
    for w in (a, a.T):
        hi = w.astype(ml_dtypes.bfloat16)
        lo = (w - hi.astype(np.float32)).astype(ml_dtypes.bfloat16)
        on_left.append(np.concatenate([hi, lo, hi], axis=1))
        on_right.append(np.concatenate([hi, lo, hi], axis=0))
    return np.stack(on_left), np.stack(on_right)


def split(x):
    hi = x.astype(jnp.bfloat16)
    return hi, (x - hi.astype(F32)).astype(jnp.bfloat16)


def left(table, x):
    hi, lo = split(x)
    return jnp.dot(table, jnp.concatenate([hi, hi, lo], axis=0), preferred_element_type=F32)


def right(x, table):
    hi, lo = split(x)
    return jnp.dot(jnp.concatenate([hi, hi, lo], axis=1), table, preferred_element_type=F32)


def swap_blocks(x, n):
    return jnp.concatenate(
        [
            jnp.concatenate([x[:n, :n], x[n:, :n]], axis=1),
            jnp.concatenate([x[:n, n:], x[n:, n:]], axis=1),
        ],
        axis=0,
    )


def tiling(nrow, n):
    tiles = 5 * (n // 8)
    half = -(-tiles // 2)
    return tiles, half, -(-half // nrow)


def place():
    return lax.axis_index("row"), lax.axis_index("col")


def remote(src, dst, send_sem, recv_sem, peer):
    return pltpu.make_async_remote_copy(
        src_ref=src, dst_ref=dst, send_sem=send_sem, recv_sem=recv_sem, device_id=peer, device_id_type=MESH
    )


def halo_kernel(nrow, ncol, n, obj_ref, ext_ref, send_sem, recv_sem, own_sem):
    _, height, width = obj_ref.shape
    blocks = width // n
    r, c = place()
    up, down = lax.rem(r + nrow - 1, nrow), lax.rem(r + 1, nrow)
    west, east = lax.rem(c + ncol - 1, ncol), lax.rem(c + 1, ncol)
    own = [
        pltpu.make_async_copy(obj_ref.at[:, :, b * n : (b + 1) * n], ext_ref.at[:, b, :height], own_sem.at[b])
        for b in range(blocks)
    ]
    barrier = pltpu.get_barrier_semaphore()
    for peer in ((up, c), (down, c), (r, west), (r, east)):
        pl.semaphore_signal(barrier, inc=1, device_id=peer, device_id_type=MESH)
    pl.semaphore_wait(barrier, 4)

    below = []
    for b in range(blocks):
        source = obj_ref.at[:, :n, b * n : (b + 1) * n]
        below.append(remote(source, ext_ref.at[:, b, height:], send_sem.at[b], recv_sem.at[b], (up, c)))
    right_halo = ext_ref.at[:, blocks, :height]
    corner_halo = ext_ref.at[:, blocks, height:]
    beside = remote(
        obj_ref.at[:, :, :n], right_halo, send_sem.at[blocks], recv_sem.at[blocks], (r, west)
    )
    corner = remote(
        ext_ref.at[:, 0, height:], corner_halo, send_sem.at[blocks + 1], recv_sem.at[blocks + 1], (r, west)
    )
    has_below, has_right = r < nrow - 1, c < ncol - 1

    @pl.when(r > 0)
    def _():
        below[0].start()

    @pl.when(c > 0)
    def _():
        beside.start()

    for one in own:
        one.start()

    @pl.when(jnp.logical_not(has_below))
    def _():
        ext_ref[:, :, height:] = jnp.zeros((2, blocks + 1, n, n), F32)

    @pl.when(jnp.logical_not(has_right))
    def _():
        ext_ref[:, blocks, :] = jnp.zeros((2, height + n, n), F32)

    @pl.when(r > 0)
    def _():
        below[0].wait_send()
        for one in below[1:]:
            one.start()

    @pl.when(has_below)
    def _():
        below[0].wait_recv()

        @pl.when(c > 0)
        def _():
            corner.start()

        for one in below[1:]:
            one.wait_recv()

    for one in own:
        one.wait()

    @pl.when(has_right)
    def _():
        beside.wait_recv()

        @pl.when(has_below)
        def _():
            corner.wait_recv()

    @pl.when(r > 0)
    def _():
        for one in below[1:]:
            one.wait_send()

    @pl.when(c > 0)
    def _():
        beside.wait_send()

        @pl.when(has_below)
        def _():
            corner.wait_send()


def compute_kernel(
    shares, group, height, width,
    pos_ref, cnt_ref, ext_ref, probe_ref, meas_ref, left_ref, right_ref, grad_ref, red_ref, sums,
):
    n = probe_ref.shape[-1]
    slots = meas_ref.shape[0]
    tiles, half, share = shares
    blocks = width // n
    pr = [probe_ref[0, 0], probe_ref[0, 1]]
    pi = [probe_ref[1, 0], probe_ref[1, 1]]
    power = pr[0] * pr[0] + pi[0] * pi[0] + (pr[1] * pr[1] + pi[1] * pi[1])
    inverse = 1.0 / (jnp.max(power, keepdims=True) + 1e-06)
    lane = lax.broadcasted_iota(jnp.int32, (n, n), 1)
    grad_ref[...] = jnp.zeros(grad_ref.shape, F32)
    grad_ref[:, :blocks, :height] = ext_ref[:, :blocks, :height]
    sums[...] = jnp.zeros(sums.shape, F32)

    def some_slots(first, carry):
        pr = [probe_ref[0, 0], probe_ref[0, 1]]
        pi = [probe_ref[1, 0], probe_ref[1, 1]]
        numbers = [first * group + k for k in range(group)]
        starts, cuts, lefts = [], [], []
        for s in numbers:
            row, col = pos_ref[0, s], pos_ref[1, s]
            near = col // n
            shift = lax.rem(col, n)
            back_shift = lax.rem(n - shift, n)
            rows = pl.ds(row, n)
            starts.append((rows, near, shift))
            patch = []
            for part in range(2):
                a = pltpu.roll(ext_ref[part, near, rows], back_shift, 1)
                b = pltpu.roll(ext_ref[part, near + 1, rows], back_shift, 1)
                patch.append(jnp.where(lane < n - shift, a, b))
            cuts.append(patch)
            qr, qi = patch
            waves = jnp.concatenate(
                [
                    jnp.concatenate([pr[m] * qr - pi[m] * qi for m in range(2)], axis=1),
                    jnp.concatenate([pr[m] * qi + pi[m] * qr for m in range(2)], axis=1),
                ],
                axis=0,
            )
            lefts.append(swap_blocks(left(left_ref[1], waves), n))
        far = right(jnp.concatenate(lefts, axis=0), right_ref[0])
        scaled = []
        for k, s in enumerate(numbers):
            live = jnp.where(s < cnt_ref[0, 0], 1.0, 0.0).astype(F32)
            mine = far[2 * n * k : 2 * n * (k + 1)]
            squares = mine * mine
            intensity = squares[:n, :n] + squares[:n, n:] + (squares[n:, :n] + squares[n:, n:])
            scaling = (meas_ref[s] * lax.rsqrt(jnp.maximum(intensity, AMP_FLOOR * AMP_FLOOR)) - 1.0) * live
            scaling = jnp.concatenate([scaling, scaling], axis=1)
            scaled.append(mine * jnp.concatenate([scaling, scaling], axis=0))
        middle = right(jnp.concatenate(scaled, axis=0), right_ref[1])
        added = [0.0] * 5
        for k, s in enumerate(numbers):
            live = jnp.where(s < cnt_ref[0, 0], 1.0, 0.0).astype(F32)
            qr, qi = cuts[k]
            rows, near, shift = starts[k]
            back = left(left_ref[0], swap_blocks(middle[2 * n * k : 2 * n * (k + 1)], n))
            br = [back[:n, :n], back[:n, n:]]
            bi = [back[n:, :n], back[n:, n:]]
            for m in range(2):
                added[m] += qr * br[m] + qi * bi[m]
                added[2 + m] += qr * bi[m] - qi * br[m]
            added[4] += live * (qr * qr + qi * qi)
            terms = (
                pr[0] * br[0] + pi[0] * bi[0] + (pr[1] * br[1] + pi[1] * bi[1]),
                pr[0] * bi[0] - pi[0] * br[0] + (pr[1] * bi[1] - pi[1] * br[1]),
            )
            for part in range(2):
                term = pltpu.roll(terms[part] * inverse, shift, 1)
                grad_ref[part, near, rows] += jnp.where(lane >= shift, term, 0.0)
                grad_ref[part, near + 1, rows] += jnp.where(lane < shift, term, 0.0)
        for ch in range(5):
            sums[ch] += added[ch]
        return carry

    lax.fori_loop(0, slots // group, some_slots, 0)
    per = n // 8
    for g in range(2 * red_ref.shape[1] * share):
        h, k = divmod(g, red_ref.shape[1] * share)
        t = h * half + k
        used = k < half and t < tiles
        value = sums[t // per, 8 * (t % per) : 8 * (t % per) + 8] if used else jnp.zeros((8, n), F32)
        red_ref[h, k // share, k % share] = value


def finish_kernel(
    nrow, ncol, n, shares,
    grad_ref, red_ref, obj_ref, every,
    got1, acc1, got2, in_right, in_corner, in_below, rim,
    send1, recv1, send2, recv2, send3, recv3, send_spill, recv_spill,
):
    _, height, width = obj_ref.shape
    tiles, half, share = shares
    blocks = width // n
    nchip = ncol // 2
    r, c = place()
    chip, core = c // 2, lax.rem(c, 2)
    down = lax.rem(r + 1, nrow)
    west, east = lax.rem(c + ncol - 1, ncol), lax.rem(c + 1, ncol)
    others = [(d, other) for d in range(nrow) for other in range(2) if d or other]
    group_peer = lambda d, other: (lax.rem(r + d, nrow), c + other * (1 - 2 * core))
    chip_peer = lambda d: (r, lax.rem(chip + d, nchip) * 2 + core)
    barrier = pltpu.get_barrier_semaphore()
    peers = [group_peer(*o) for o in others] + [chip_peer(d) for d in range(1, nchip)]
    peers += [(r, west), (r, east)]
    for peer in peers:
        pl.semaphore_signal(barrier, inc=1, device_id=peer, device_id_type=MESH)
    pl.semaphore_wait(barrier, len(peers))

    first = []
    for d, other in others:
        peer = group_peer(d, other)
        half_of = core + other * (1 - 2 * core)
        first.append(
            remote(red_ref.at[half_of, peer[0]], got1.at[core, r], send1.at[other, d], recv1.at[other, d], peer)
        )
        first[-1].start()

    corner = remote(grad_ref.at[:, blocks, height:], in_corner, send_spill.at[0], recv_spill.at[0], (r, east))
    beside = remote(grad_ref.at[:, blocks, :height], in_right, send_spill.at[1], recv_spill.at[1], (r, east))
    below = [
        remote(
            rim if b == 0 else grad_ref.at[:, b, height:],
            in_below.at[:, b], send_spill.at[2 + b], recv_spill.at[2 + b], (down, c),
        )
        for b in range(blocks)
    ]

    @pl.when(c < ncol - 1)
    def _():
        corner.start()
        beside.start()

    for b in range(blocks):
        obj_ref[:, :, b * n : (b + 1) * n] = grad_ref[:, b, :height]
    rim[...] = grad_ref[:, 0, height:]

    for one in first:
        one.wait_recv()

    @pl.when(r < nrow - 1)
    def _():
        for one in below[1:]:
            one.start()

    total = red_ref[core, r]
    for d, other in others:
        total = total + got1[core + other * (1 - 2 * core), lax.rem(r + nrow - d, nrow)]
    acc1[...] = total

    second = []
    for d in range(1, nchip):
        second.append(remote(acc1, got2.at[chip], send2.at[d], recv2.at[d], chip_peer(d)))
        second[-1].start()
    got2[chip] = total

    @pl.when(c > 0)
    def _():
        corner.wait_recv()
        rim[...] += in_corner[...]

    @pl.when(r < nrow - 1)
    def _():
        below[0].start()

    for one in second:
        one.wait_recv()
    total = got2[0]
    for k in range(1, nchip):
        total = total + got2[k]
    every[core, r] = total

    third = []
    for d, other in others:
        piece = every.at[core, r]
        third.append(remote(piece, piece, send3.at[other, d], recv3.at[other, d], group_peer(d, other)))
        third[-1].start()

    @pl.when(c > 0)
    def _():
        beside.wait_recv()
        obj_ref[:, :, :n] += in_right[...]

    @pl.when(r > 0)
    def _():
        for b, one in enumerate(below):
            one.wait_recv()
            obj_ref[:, :n, b * n : (b + 1) * n] += in_below[:, b]

    for one in third:
        one.wait_recv()

    for one in first + second + third:
        one.wait_send()

    @pl.when(c < ncol - 1)
    def _():
        corner.wait_send()
        beside.wait_send()

    @pl.when(r < nrow - 1)
    def _():
        for one in below:
            one.wait_send()


def result_kernel(shares, obj_ref, every, object_out, probe_out, probe, sems):
    tiles, half, share = shares
    n = probe.shape[-1]
    per = n // 8
    objects = pltpu.make_async_copy(obj_ref, object_out, sems.at[0])
    objects.start()

    def tile(g):
        k = g % half
        return every[g // half, k // share, k % share]

    for i in range(per):
        factor = lax.rsqrt(tile(4 * per + i) + 1.0)
        for ch in range(4):
            probe[ch // 2, ch % 2, 8 * i : 8 * i + 8] = tile(ch * per + i) * factor
    steps = pltpu.make_async_copy(probe, probe_out, sems.at[1])
    steps.start()
    objects.wait()
    steps.wait()


def per_device(nrow, ncol, tables, object_field, probe_modes, measured, positions, counts):
    n = probe_modes.shape[-1]
    _, height, width = object_field.shape
    blocks, slots = width // n, measured.shape[2]
    shares = tiles, half, share = tiling(nrow, n)
    group = 8 if slots % 8 == 0 else 1
    params = functools.partial(pltpu.CompilerParams, vmem_limit_bytes=LIMIT)
    dma = pltpu.SemaphoreType.DMA
    extended = pl.pallas_call(
        functools.partial(halo_kernel, nrow, ncol, n),
        out_shape=jax.ShapeDtypeStruct((2, blocks + 1, height + n, n), F32),
        in_specs=[HBM],
        out_specs=VMEM,
        scratch_shapes=[dma((blocks + 2,)), dma((blocks + 2,)), dma((blocks,))],
        compiler_params=params(collective_id=0, has_side_effects=True),
    )(object_field)
    gradient, sums = pl.pallas_call(
        functools.partial(compute_kernel, shares, group, height, width),
        out_shape=(
            jax.ShapeDtypeStruct((2, blocks + 1, height + n, n), F32),
            jax.ShapeDtypeStruct((2, nrow, share, 8, n), F32),
        ),
        in_specs=[SMEM, SMEM] + [VMEM] * 5,
        out_specs=(VMEM, VMEM),
        scratch_shapes=[pltpu.VMEM((5, n, n), F32)],
        compiler_params=params(),
    )(positions[0, 0], counts, extended, probe_modes, measured[0, 0], *tables)
    object_new, total = pl.pallas_call(
        functools.partial(finish_kernel, nrow, ncol, n, shares),
        out_shape=(
            jax.ShapeDtypeStruct((2, height, width), F32),
            jax.ShapeDtypeStruct((2, nrow, share, 8, n), F32),
        ),
        in_specs=[VMEM, VMEM],
        out_specs=(VMEM, VMEM),
        scratch_shapes=[
            pltpu.VMEM((2, nrow, share, 8, n), F32),
            pltpu.VMEM((share, 8, n), F32),
            pltpu.VMEM((ncol // 2, share, 8, n), F32),
            pltpu.VMEM((2, height, n), F32),
            pltpu.VMEM((2, n, n), F32),
            pltpu.VMEM((2, blocks, n, n), F32),
            pltpu.VMEM((2, n, n), F32),
        ]
        + [dma(k)
            for k in ((2, nrow), (ncol // 2,), (2, nrow), (2 + blocks,))
            for _ in range(2)
        ],
        compiler_params=params(collective_id=1, has_side_effects=True),
    )(gradient, sums)
    return pl.pallas_call(
        functools.partial(result_kernel, shares),
        out_shape=(
            jax.ShapeDtypeStruct((2, height, width), F32),
            jax.ShapeDtypeStruct((2, 2, n, n), F32),
        ),
        in_specs=[VMEM, VMEM],
        out_specs=(HBM, HBM),
        scratch_shapes=[pltpu.VMEM((2, 2, n, n), F32), dma((2,))],
        compiler_params=params(),
    )(object_new, total)


def solution(mesh):
    nrow, ncol = mesh.shape["row"], mesh.shape["col"]
    in_specs = (
        P(None, "row", "col"),
        P(),
        P("row", "col", None, None, None),
        P("row", "col", None, None),
        P("row", "col"),
    )
    out_specs = (P(None, "row", "col"), P())

    def run(object_field, probe_modes, measured, positions, counts):
        tables = [jnp.asarray(t) for t in fourier_tables(probe_modes.shape[-1])]
        return jax.shard_map(
            functools.partial(per_device, nrow, ncol, tables),
            mesh=mesh, in_specs=in_specs, out_specs=out_specs, check_vma=False,
        )(object_field, probe_modes, measured, positions, counts)

    return run
```

```python
import functools
import math

import jax
import jax.numpy as jnp
import ml_dtypes
import numpy as np
from jax import lax
from jax.experimental import pallas as pl
from jax.experimental.pallas import tpu as pltpu
from jax.sharding import PartitionSpec as P

AMP_FLOOR = 0.25
F32 = jnp.float32
MESH = pl.DeviceIdType.MESH
VMEM = pl.BlockSpec(memory_space=pltpu.VMEM)
SMEM = pl.BlockSpec(memory_space=pltpu.SMEM)
HBM = pl.BlockSpec(memory_space=pltpu.HBM)
LIMIT = 48 * 1024 * 1024


def fourier_tables(n):
    index = np.arange(n)
    angle = (index[:, None] * index[None, :] % n) * (2.0 * math.pi / n)
    c = np.cos(angle) / math.sqrt(n)
    s = np.sin(angle) / math.sqrt(n)
    a = np.block([[c, -s], [s, c]]).astype(np.float32)
    on_left, on_right = [], []
    for w in (a, a.T):
        hi = w.astype(ml_dtypes.bfloat16)
        lo = (w - hi.astype(np.float32)).astype(ml_dtypes.bfloat16)
        on_left.append(np.concatenate([hi, lo, hi], axis=1))
        on_right.append(np.concatenate([hi, lo, hi], axis=0))
    return np.stack(on_left), np.stack(on_right)


def split(x):
    hi = x.astype(jnp.bfloat16)
    return hi, (x - hi.astype(F32)).astype(jnp.bfloat16)


def left(table, x):
    hi, lo = split(x)
    return jnp.dot(table, jnp.concatenate([hi, hi, lo], axis=0), preferred_element_type=F32)


def right(x, table):
    hi, lo = split(x)
    return jnp.dot(jnp.concatenate([hi, hi, lo], axis=1), table, preferred_element_type=F32)


def swap_blocks(x, n):
    return jnp.concatenate(
        [
            jnp.concatenate([x[:n, :n], x[n:, :n]], axis=1),
            jnp.concatenate([x[:n, n:], x[n:, n:]], axis=1),
        ],
        axis=0,
    )


def tiling(nrow, n):
    tiles = 5 * (n // 8)
    half = -(-tiles // 2)
    return tiles, half, -(-half // nrow)


def place():
    return lax.axis_index("row"), lax.axis_index("col")


def remote(src, dst, send_sem, recv_sem, peer):
    return pltpu.make_async_remote_copy(
        src_ref=src, dst_ref=dst, send_sem=send_sem, recv_sem=recv_sem, device_id=peer, device_id_type=MESH
    )


def halo_kernel(nrow, ncol, n, obj_ref, ext_ref, send_sem, recv_sem, own_sem):
    _, height, width = obj_ref.shape
    blocks = width // n
    r, c = place()
    up, down = lax.rem(r + nrow - 1, nrow), lax.rem(r + 1, nrow)
    west, east = lax.rem(c + ncol - 1, ncol), lax.rem(c + 1, ncol)
    own = [
        pltpu.make_async_copy(obj_ref.at[:, :, b * n : (b + 1) * n], ext_ref.at[:, b, :height], own_sem.at[b])
        for b in range(blocks)
    ]
    barrier = pltpu.get_barrier_semaphore()
    for peer in ((up, c), (down, c), (r, west), (r, east)):
        pl.semaphore_signal(barrier, inc=1, device_id=peer, device_id_type=MESH)
    pl.semaphore_wait(barrier, 4)

    below = []
    for b in range(blocks):
        source = obj_ref.at[:, :n, b * n : (b + 1) * n]
        below.append(remote(source, ext_ref.at[:, b, height:], send_sem.at[b], recv_sem.at[b], (up, c)))
    right_halo = ext_ref.at[:, blocks, :height]
    corner_halo = ext_ref.at[:, blocks, height:]
    beside = remote(
        obj_ref.at[:, :, :n], right_halo, send_sem.at[blocks], recv_sem.at[blocks], (r, west)
    )
    corner = remote(
        ext_ref.at[:, 0, height:], corner_halo, send_sem.at[blocks + 1], recv_sem.at[blocks + 1], (r, west)
    )
    has_below, has_right = r < nrow - 1, c < ncol - 1

    @pl.when(r > 0)
    def _():
        below[0].start()

    @pl.when(c > 0)
    def _():
        beside.start()

    for one in own:
        one.start()

    @pl.when(jnp.logical_not(has_below))
    def _():
        ext_ref[:, :, height:] = jnp.zeros((2, blocks + 1, n, n), F32)

    @pl.when(jnp.logical_not(has_right))
    def _():
        ext_ref[:, blocks, :] = jnp.zeros((2, height + n, n), F32)

    @pl.when(r > 0)
    def _():
        below[0].wait_send()
        for one in below[1:]:
            one.start()

    @pl.when(has_below)
    def _():
        below[0].wait_recv()

        @pl.when(c > 0)
        def _():
            corner.start()

        for one in below[1:]:
            one.wait_recv()

    for one in own:
        one.wait()

    @pl.when(has_right)
    def _():
        beside.wait_recv()

        @pl.when(has_below)
        def _():
            corner.wait_recv()

    @pl.when(r > 0)
    def _():
        for one in below[1:]:
            one.wait_send()

    @pl.when(c > 0)
    def _():
        beside.wait_send()

        @pl.when(has_below)
        def _():
            corner.wait_send()


def compute_kernel(
    shares, group, height, width,
    pos_ref, cnt_ref, ext_ref, probe_ref, meas_ref, left_ref, right_ref, grad_ref, red_ref, sums,
):
    n = probe_ref.shape[-1]
    slots = meas_ref.shape[0]
    tiles, half, share = shares
    blocks = width // n
    pr = [probe_ref[0, 0], probe_ref[0, 1]]
    pi = [probe_ref[1, 0], probe_ref[1, 1]]
    power = pr[0] * pr[0] + pi[0] * pi[0] + (pr[1] * pr[1] + pi[1] * pi[1])
    inverse = 1.0 / (jnp.max(power, keepdims=True) + 1e-06)
    lane = lax.broadcasted_iota(jnp.int32, (n, n), 1)
    grad_ref[...] = jnp.zeros(grad_ref.shape, F32)
    grad_ref[:, :blocks, :height] = ext_ref[:, :blocks, :height]
    sums[...] = jnp.zeros(sums.shape, F32)

    def some_slots(first, carry):
        pr = [probe_ref[0, 0], probe_ref[0, 1]]
        pi = [probe_ref[1, 0], probe_ref[1, 1]]
        numbers = [first * group + k for k in range(group)]
        starts, cuts, lefts = [], [], []
        for s in numbers:
            row, col = pos_ref[0, s], pos_ref[1, s]
            near = col // n
            shift = lax.rem(col, n)
            back_shift = lax.rem(n - shift, n)
            rows = pl.ds(row, n)
            starts.append((rows, near, shift))
            patch = []
            for part in range(2):
                a = pltpu.roll(ext_ref[part, near, rows], back_shift, 1)
                b = pltpu.roll(ext_ref[part, near + 1, rows], back_shift, 1)
                patch.append(jnp.where(lane < n - shift, a, b))
            cuts.append(patch)
            qr, qi = patch
            waves = jnp.concatenate(
                [
                    jnp.concatenate([pr[m] * qr - pi[m] * qi for m in range(2)], axis=1),
                    jnp.concatenate([pr[m] * qi + pi[m] * qr for m in range(2)], axis=1),
                ],
                axis=0,
            )
            lefts.append(swap_blocks(left(left_ref[1], waves), n))
        far = right(jnp.concatenate(lefts, axis=0), right_ref[0])
        scaled = []
        for k, s in enumerate(numbers):
            live = jnp.where(s < cnt_ref[0, 0], 1.0, 0.0).astype(F32)
            mine = far[2 * n * k : 2 * n * (k + 1)]
            squares = mine * mine
            intensity = squares[:n, :n] + squares[:n, n:] + (squares[n:, :n] + squares[n:, n:])
            scaling = (meas_ref[s] * lax.rsqrt(jnp.maximum(intensity, AMP_FLOOR * AMP_FLOOR)) - 1.0) * live
            scaling = jnp.concatenate([scaling, scaling], axis=1)
            scaled.append(mine * jnp.concatenate([scaling, scaling], axis=0))
        middle = right(jnp.concatenate(scaled, axis=0), right_ref[1])
        added = [0.0] * 5
        for k, s in enumerate(numbers):
            live = jnp.where(s < cnt_ref[0, 0], 1.0, 0.0).astype(F32)
            qr, qi = cuts[k]
            rows, near, shift = starts[k]
            back = left(left_ref[0], swap_blocks(middle[2 * n * k : 2 * n * (k + 1)], n))
            br = [back[:n, :n], back[:n, n:]]
            bi = [back[n:, :n], back[n:, n:]]
            for m in range(2):
                added[m] += qr * br[m] + qi * bi[m]
                added[2 + m] += qr * bi[m] - qi * br[m]
            added[4] += live * (qr * qr + qi * qi)
            terms = (
                pr[0] * br[0] + pi[0] * bi[0] + (pr[1] * br[1] + pi[1] * bi[1]),
                pr[0] * bi[0] - pi[0] * br[0] + (pr[1] * bi[1] - pi[1] * br[1]),
            )
            for part in range(2):
                term = pltpu.roll(terms[part] * inverse, shift, 1)
                grad_ref[part, near, rows] += jnp.where(lane >= shift, term, 0.0)
                grad_ref[part, near + 1, rows] += jnp.where(lane < shift, term, 0.0)
        for ch in range(5):
            sums[ch] += added[ch]
        return carry

    lax.fori_loop(0, slots // group, some_slots, 0)
    per = n // 8
    for g in range(2 * red_ref.shape[1] * share):
        h, k = divmod(g, red_ref.shape[1] * share)
        t = h * half + k
        used = k < half and t < tiles
        value = sums[t // per, 8 * (t % per) : 8 * (t % per) + 8] if used else jnp.zeros((8, n), F32)
        red_ref[h, k // share, k % share] = value


def finish_kernel(
    nrow, ncol, n, shares,
    grad_ref, red_ref, obj_ref, every,
    got0, acc0, got1, acc1, got2, in_right, in_corner, in_below, rim,
    send0, recv0, send1, recv1, send2, recv2, send3, recv3, send4, recv4, send_spill, recv_spill,
):
    _, height, width = obj_ref.shape
    tiles, half, share = shares
    blocks = width // n
    nchip = ncol // 2
    r, c = place()
    chip, core = c // 2, lax.rem(c, 2)
    down = lax.rem(r + 1, nrow)
    west, east = lax.rem(c + ncol - 1, ncol), lax.rem(c + 1, ncol)
    twin = (r, c + 1 - 2 * core)
    row_peer = lambda d: (lax.rem(r + d, nrow), c)
    chip_peer = lambda d: (r, lax.rem(chip + d, nchip) * 2 + core)
    barrier = pltpu.get_barrier_semaphore()
    peers = [row_peer(d) for d in range(1, nrow)] + [chip_peer(d) for d in range(1, nchip)]
    peers += [(r, west), (r, east)]
    for peer in peers:
        pl.semaphore_signal(barrier, inc=1, device_id=peer, device_id_type=MESH)
    pl.semaphore_wait(barrier, len(peers))

    pair = remote(red_ref.at[1 - core], got0, send0.at[0], recv0.at[0], twin)
    pair.start()

    corner = remote(grad_ref.at[:, blocks, height:], in_corner, send_spill.at[0], recv_spill.at[0], (r, east))
    beside = remote(grad_ref.at[:, blocks, :height], in_right, send_spill.at[1], recv_spill.at[1], (r, east))
    below = [
        remote(
            rim.at[part] if b == 0 else grad_ref.at[part, b, height:],
            in_below.at[part, b], send_spill.at[2 + 2 * b + part], recv_spill.at[2 + 2 * b + part], (down, c),
        )
        for b in range(blocks)
        for part in range(2)
    ]
    early, late = below[2::2], below[3::2]

    @pl.when(c < ncol - 1)
    def _():
        corner.start()
        beside.start()

    @pl.when(r < nrow - 1)
    def _():
        for one in early:
            one.start()

    pair.wait_recv()
    acc0[...] = red_ref[core] + got0[...]
    first = []
    for d in range(1, nrow):
        peer = row_peer(d)
        first.append(remote(acc0.at[peer[0]], got1.at[r], send1.at[d], recv1.at[d], peer))
        first[-1].start()

    for b in range(blocks):
        obj_ref[:, :, b * n : (b + 1) * n] = grad_ref[:, b, :height]
    rim[...] = grad_ref[:, 0, height:]

    for one in first:
        one.wait_recv()

    @pl.when(r < nrow - 1)
    def _():
        for one in late:
            one.start()

    total = acc0[r]
    for d in range(1, nrow):
        total = total + got1[lax.rem(r + nrow - d, nrow)]
    acc1[...] = total

    second = []
    for d in range(1, nchip):
        second.append(remote(acc1, got2.at[chip], send2.at[d], recv2.at[d], chip_peer(d)))
        second[-1].start()
    got2[chip] = total

    @pl.when(c > 0)
    def _():
        corner.wait_recv()
        rim[...] += in_corner[...]

    @pl.when(r < nrow - 1)
    def _():
        for one in below[:2]:
            one.start()

    for one in second:
        one.wait_recv()
    total = got2[0]
    for k in range(1, nchip):
        total = total + got2[k]
    every[core, r] = total

    third = []
    for d in range(1, nrow):
        piece = every.at[core, r]
        third.append(remote(piece, piece, send3.at[d], recv3.at[d], row_peer(d)))
        third[-1].start()

    @pl.when(c > 0)
    def _():
        beside.wait_recv()
        obj_ref[:, :, :n] += in_right[...]

    for one in third:
        one.wait_recv()
    fourth = remote(every.at[core], every.at[core], send4.at[0], recv4.at[0], twin)
    fourth.start()

    @pl.when(r > 0)
    def _():
        for one in below[2:] + below[:2]:
            one.wait_recv()
        for b in range(blocks):
            obj_ref[:, :n, b * n : (b + 1) * n] += in_below[:, b]

    fourth.wait_recv()

    for one in [pair] + first + second + third + [fourth]:
        one.wait_send()

    @pl.when(c < ncol - 1)
    def _():
        corner.wait_send()
        beside.wait_send()

    @pl.when(r < nrow - 1)
    def _():
        for one in below:
            one.wait_send()


def result_kernel(shares, obj_ref, every, object_out, probe_out, probe, sems):
    tiles, half, share = shares
    n = probe.shape[-1]
    per = n // 8
    objects = pltpu.make_async_copy(obj_ref, object_out, sems.at[0])
    objects.start()

    def tile(g):
        k = g % half
        return every[g // half, k // share, k % share]

    for i in range(per):
        factor = lax.rsqrt(tile(4 * per + i) + 1.0)
        for ch in range(4):
            probe[ch // 2, ch % 2, 8 * i : 8 * i + 8] = tile(ch * per + i) * factor
    steps = pltpu.make_async_copy(probe, probe_out, sems.at[1])
    steps.start()
    objects.wait()
    steps.wait()


def per_device(nrow, ncol, tables, object_field, probe_modes, measured, positions, counts):
    n = probe_modes.shape[-1]
    _, height, width = object_field.shape
    blocks, slots = width // n, measured.shape[2]
    shares = tiles, half, share = tiling(nrow, n)
    group = 8 if slots % 8 == 0 else 1
    params = functools.partial(pltpu.CompilerParams, vmem_limit_bytes=LIMIT)
    dma = pltpu.SemaphoreType.DMA
    extended = pl.pallas_call(
        functools.partial(halo_kernel, nrow, ncol, n),
        out_shape=jax.ShapeDtypeStruct((2, blocks + 1, height + n, n), F32),
        in_specs=[HBM],
        out_specs=VMEM,
        scratch_shapes=[dma((blocks + 2,)), dma((blocks + 2,)), dma((blocks,))],
        compiler_params=params(collective_id=0, has_side_effects=True),
    )(object_field)
    gradient, sums = pl.pallas_call(
        functools.partial(compute_kernel, shares, group, height, width),
        out_shape=(
            jax.ShapeDtypeStruct((2, blocks + 1, height + n, n), F32),
            jax.ShapeDtypeStruct((2, nrow, share, 8, n), F32),
        ),
        in_specs=[SMEM, SMEM] + [VMEM] * 5,
        out_specs=(VMEM, VMEM),
        scratch_shapes=[pltpu.VMEM((5, n, n), F32)],
        compiler_params=params(),
    )(positions[0, 0], counts, extended, probe_modes, measured[0, 0], *tables)
    object_new, total = pl.pallas_call(
        functools.partial(finish_kernel, nrow, ncol, n, shares),
        out_shape=(
            jax.ShapeDtypeStruct((2, height, width), F32),
            jax.ShapeDtypeStruct((2, nrow, share, 8, n), F32),
        ),
        in_specs=[VMEM, VMEM],
        out_specs=(VMEM, VMEM),
        scratch_shapes=[
            pltpu.VMEM((nrow, share, 8, n), F32),
            pltpu.VMEM((nrow, share, 8, n), F32),
            pltpu.VMEM((nrow, share, 8, n), F32),
            pltpu.VMEM((share, 8, n), F32),
            pltpu.VMEM((ncol // 2, share, 8, n), F32),
            pltpu.VMEM((2, height, n), F32),
            pltpu.VMEM((2, n, n), F32),
            pltpu.VMEM((2, blocks, n, n), F32),
            pltpu.VMEM((2, n, n), F32),
        ]
        + [dma((k,)) for k in (1, 1, nrow, nrow, ncol // 2, ncol // 2, nrow, nrow, 1, 1, 2 + 2 * blocks, 2 + 2 * blocks)],
        compiler_params=params(collective_id=1, has_side_effects=True),
    )(gradient, sums)
    return pl.pallas_call(
        functools.partial(result_kernel, shares),
        out_shape=(
            jax.ShapeDtypeStruct((2, height, width), F32),
            jax.ShapeDtypeStruct((2, 2, n, n), F32),
        ),
        in_specs=[VMEM, VMEM],
        out_specs=(HBM, HBM),
        scratch_shapes=[pltpu.VMEM((2, 2, n, n), F32), dma((2,))],
        compiler_params=params(),
    )(object_new, total)


def solution(mesh):
    nrow, ncol = mesh.shape["row"], mesh.shape["col"]
    in_specs = (
        P(None, "row", "col"),
        P(),
        P("row", "col", None, None, None),
        P("row", "col", None, None),
        P("row", "col"),
    )
    out_specs = (P(None, "row", "col"), P())

    def run(object_field, probe_modes, measured, positions, counts):
        tables = [jnp.asarray(t) for t in fourier_tables(probe_modes.shape[-1])]
        return jax.shard_map(
            functools.partial(per_device, nrow, ncol, tables),
            mesh=mesh, in_specs=in_specs, out_specs=out_specs, check_vma=False,
        )(object_field, probe_modes, measured, positions, counts)

    return run
```

```python
import functools
import math

import jax
import jax.numpy as jnp
import ml_dtypes
import numpy as np
from jax import lax
from jax.experimental import pallas as pl
from jax.experimental.pallas import tpu as pltpu
from jax.sharding import PartitionSpec as P

AMP_FLOOR = 0.25
F32 = jnp.float32
MESH = pl.DeviceIdType.MESH
VMEM = pl.BlockSpec(memory_space=pltpu.VMEM)
SMEM = pl.BlockSpec(memory_space=pltpu.SMEM)
HBM = pl.BlockSpec(memory_space=pltpu.HBM)
LIMIT = 48 * 1024 * 1024


def fourier_tables(n):
    index = np.arange(n)
    angle = (index[:, None] * index[None, :] % n) * (2.0 * math.pi / n)
    c = np.cos(angle) / math.sqrt(n)
    s = np.sin(angle) / math.sqrt(n)
    a = np.block([[c, -s], [s, c]]).astype(np.float32)
    on_left, on_right = [], []
    for w in (a, a.T):
        hi = w.astype(ml_dtypes.bfloat16)
        lo = (w - hi.astype(np.float32)).astype(ml_dtypes.bfloat16)
        on_left.append(np.concatenate([hi, lo, hi], axis=1))
        on_right.append(np.concatenate([hi, lo, hi], axis=0))
    return np.stack(on_left), np.stack(on_right)


def split(x):
    hi = x.astype(jnp.bfloat16)
    return hi, (x - hi.astype(F32)).astype(jnp.bfloat16)


def left(table, x):
    hi, lo = split(x)
    return jnp.dot(table, jnp.concatenate([hi, hi, lo], axis=0), preferred_element_type=F32)


def right(x, table):
    hi, lo = split(x)
    return jnp.dot(jnp.concatenate([hi, hi, lo], axis=1), table, preferred_element_type=F32)


def swap_blocks(x, n):
    return jnp.concatenate(
        [
            jnp.concatenate([x[:n, :n], x[n:, :n]], axis=1),
            jnp.concatenate([x[:n, n:], x[n:, n:]], axis=1),
        ],
        axis=0,
    )


def tiling(nrow, n):
    tiles = 5 * (n // 8)
    half = -(-tiles // 2)
    return tiles, half, -(-half // nrow)


def place():
    return lax.axis_index("row"), lax.axis_index("col")


def remote(src, dst, send_sem, recv_sem, peer):
    return pltpu.make_async_remote_copy(
        src_ref=src, dst_ref=dst, send_sem=send_sem, recv_sem=recv_sem, device_id=peer, device_id_type=MESH
    )


def halo_kernel(nrow, ncol, n, obj_ref, ext_ref, send_sem, recv_sem, own_sem):
    _, height, width = obj_ref.shape
    blocks = width // n
    r, c = place()
    up, down = lax.rem(r + nrow - 1, nrow), lax.rem(r + 1, nrow)
    west, east = lax.rem(c + ncol - 1, ncol), lax.rem(c + 1, ncol)
    own = [
        pltpu.make_async_copy(obj_ref.at[:, :, b * n : (b + 1) * n], ext_ref.at[:, b, :height], own_sem.at[b])
        for b in range(blocks)
    ]
    barrier = pltpu.get_barrier_semaphore()
    @pl.when(r < nrow - 1)
    def _():
        pl.semaphore_signal(barrier, inc=1, device_id=(down, c), device_id_type=MESH)

    @pl.when(c < ncol - 1)
    def _():
        pl.semaphore_signal(barrier, inc=1, device_id=(r, east), device_id_type=MESH)

    @pl.when(r + c > 0)
    def _():
        pl.semaphore_wait(barrier, jnp.minimum(r, 1) + jnp.minimum(c, 1))

    below = []
    for b in range(blocks):
        source = obj_ref.at[:, :n, b * n : (b + 1) * n]
        below.append(remote(source, ext_ref.at[:, b, height:], send_sem.at[b], recv_sem.at[b], (up, c)))
    right_halo = ext_ref.at[:, blocks, :height]
    corner_halo = ext_ref.at[:, blocks, height:]
    beside = remote(
        obj_ref.at[:, :, :n], right_halo, send_sem.at[blocks], recv_sem.at[blocks], (r, west)
    )
    corner = remote(
        ext_ref.at[:, 0, height:], corner_halo, send_sem.at[blocks + 1], recv_sem.at[blocks + 1], (r, west)
    )
    has_below, has_right = r < nrow - 1, c < ncol - 1

    @pl.when(r > 0)
    def _():
        below[0].start()

    @pl.when(c > 0)
    def _():
        beside.start()

    for one in own:
        one.start()

    @pl.when(jnp.logical_not(has_below))
    def _():
        ext_ref[:, :, height:] = jnp.zeros((2, blocks + 1, n, n), F32)

    @pl.when(jnp.logical_not(has_right))
    def _():
        ext_ref[:, blocks, :] = jnp.zeros((2, height + n, n), F32)

    @pl.when(r > 0)
    def _():
        below[0].wait_send()
        for one in below[1:]:
            one.start()

    @pl.when(has_below)
    def _():
        below[0].wait_recv()

        @pl.when(c > 0)
        def _():
            corner.start()

        for one in below[1:]:
            one.wait_recv()

    for one in own:
        one.wait()

    @pl.when(has_right)
    def _():
        beside.wait_recv()

        @pl.when(has_below)
        def _():
            corner.wait_recv()

    @pl.when(r > 0)
    def _():
        for one in below[1:]:
            one.wait_send()

    @pl.when(c > 0)
    def _():
        beside.wait_send()

        @pl.when(has_below)
        def _():
            corner.wait_send()


def compute_kernel(
    shares, group, height, width,
    pos_ref, cnt_ref, ext_ref, probe_ref, meas_ref, left_ref, right_ref, grad_ref, red_ref, sums,
):
    n = probe_ref.shape[-1]
    slots = meas_ref.shape[0]
    tiles, half, share = shares
    blocks = width // n
    pr = [probe_ref[0, 0], probe_ref[0, 1]]
    pi = [probe_ref[1, 0], probe_ref[1, 1]]
    power = pr[0] * pr[0] + pi[0] * pi[0] + (pr[1] * pr[1] + pi[1] * pi[1])
    inverse = 1.0 / (jnp.max(power, keepdims=True) + 1e-06)
    lane = lax.broadcasted_iota(jnp.int32, (n, n), 1)
    grad_ref[...] = jnp.zeros(grad_ref.shape, F32)
    grad_ref[:, :blocks, :height] = ext_ref[:, :blocks, :height]
    sums[...] = jnp.zeros(sums.shape, F32)

    def some_slots(first, carry):
        pr = [probe_ref[0, 0], probe_ref[0, 1]]
        pi = [probe_ref[1, 0], probe_ref[1, 1]]
        numbers = [first * group + k for k in range(group)]
        starts, cuts, lefts = [], [], []
        for s in numbers:
            row, col = pos_ref[0, s], pos_ref[1, s]
            near = col // n
            shift = lax.rem(col, n)
            back_shift = lax.rem(n - shift, n)
            rows = pl.ds(row, n)
            starts.append((rows, near, shift))
            patch = []
            for part in range(2):
                a = pltpu.roll(ext_ref[part, near, rows], back_shift, 1)
                b = pltpu.roll(ext_ref[part, near + 1, rows], back_shift, 1)
                patch.append(jnp.where(lane < n - shift, a, b))
            cuts.append(patch)
            qr, qi = patch
            waves = jnp.concatenate(
                [
                    jnp.concatenate([pr[m] * qr - pi[m] * qi for m in range(2)], axis=1),
                    jnp.concatenate([pr[m] * qi + pi[m] * qr for m in range(2)], axis=1),
                ],
                axis=0,
            )
            lefts.append(swap_blocks(left(left_ref[1], waves), n))
        far = right(jnp.concatenate(lefts, axis=0), right_ref[0])
        scaled = []
        for k, s in enumerate(numbers):
            live = jnp.where(s < cnt_ref[0, 0], 1.0, 0.0).astype(F32)
            mine = far[2 * n * k : 2 * n * (k + 1)]
            squares = mine * mine
            intensity = squares[:n, :n] + squares[:n, n:] + (squares[n:, :n] + squares[n:, n:])
            scaling = (meas_ref[s] * lax.rsqrt(jnp.maximum(intensity, AMP_FLOOR * AMP_FLOOR)) - 1.0) * live
            scaling = jnp.concatenate([scaling, scaling], axis=1)
            scaled.append(mine * jnp.concatenate([scaling, scaling], axis=0))
        middle = right(jnp.concatenate(scaled, axis=0), right_ref[1])
        added = [0.0] * 5
        for k, s in enumerate(numbers):
            live = jnp.where(s < cnt_ref[0, 0], 1.0, 0.0).astype(F32)
            qr, qi = cuts[k]
            rows, near, shift = starts[k]
            back = left(left_ref[0], swap_blocks(middle[2 * n * k : 2 * n * (k + 1)], n))
            br = [back[:n, :n], back[:n, n:]]
            bi = [back[n:, :n], back[n:, n:]]
            for m in range(2):
                added[m] += qr * br[m] + qi * bi[m]
                added[2 + m] += qr * bi[m] - qi * br[m]
            added[4] += live * (qr * qr + qi * qi)
            terms = (
                pr[0] * br[0] + pi[0] * bi[0] + (pr[1] * br[1] + pi[1] * bi[1]),
                pr[0] * bi[0] - pi[0] * br[0] + (pr[1] * bi[1] - pi[1] * br[1]),
            )
            for part in range(2):
                term = pltpu.roll(terms[part] * inverse, shift, 1)
                grad_ref[part, near, rows] += jnp.where(lane >= shift, term, 0.0)
                grad_ref[part, near + 1, rows] += jnp.where(lane < shift, term, 0.0)
        for ch in range(5):
            sums[ch] += added[ch]
        return carry

    lax.fori_loop(0, slots // group, some_slots, 0)
    per = n // 8
    for g in range(2 * red_ref.shape[1] * share):
        h, k = divmod(g, red_ref.shape[1] * share)
        t = h * half + k
        used = k < half and t < tiles
        value = sums[t // per, 8 * (t % per) : 8 * (t % per) + 8] if used else jnp.zeros((8, n), F32)
        red_ref[h, k // share, k % share] = value


def finish_kernel(
    nrow, ncol, n, shares,
    grad_ref, red_ref, obj_ref, every,
    got0, acc0, got1, acc1, got2, in_right, in_corner, in_below, rim,
    send0, recv0, send1, recv1, send2, recv2, send3, recv3, send4, recv4, send_spill, recv_spill,
):
    _, height, width = obj_ref.shape
    tiles, half, share = shares
    blocks = width // n
    nchip = ncol // 2
    r, c = place()
    chip, core = c // 2, lax.rem(c, 2)
    down = lax.rem(r + 1, nrow)
    west, east = lax.rem(c + ncol - 1, ncol), lax.rem(c + 1, ncol)
    twin = (r, c + 1 - 2 * core)
    row_peer = lambda d: (lax.rem(r + d, nrow), c)
    chip_peer = lambda d: (r, lax.rem(chip + d, nchip) * 2 + core)
    barrier = pltpu.get_barrier_semaphore()
    peers = [row_peer(d) for d in range(1, nrow)] + [chip_peer(d) for d in range(1, nchip)]
    peers += [twin]
    for peer in peers:
        pl.semaphore_signal(barrier, inc=1, device_id=peer, device_id_type=MESH)

    @pl.when((core == 0) & (c > 0))
    def _():
        pl.semaphore_signal(barrier, inc=1, device_id=(r, west), device_id_type=MESH)

    pl.semaphore_wait(barrier, len(peers) + core * jnp.minimum(ncol - 1 - c, 1))

    pair = remote(red_ref.at[1 - core], got0, send0.at[0], recv0.at[0], twin)
    pair.start()

    corner = remote(grad_ref.at[:, blocks, height:], in_corner, send_spill.at[0], recv_spill.at[0], (r, east))
    beside = remote(grad_ref.at[:, blocks, :height], in_right, send_spill.at[1], recv_spill.at[1], (r, east))
    below = [
        remote(
            rim if b == 0 else grad_ref.at[:, b, height:],
            in_below.at[:, b], send_spill.at[2 + b], recv_spill.at[2 + b], (down, c),
        )
        for b in range(blocks)
    ]

    @pl.when(c < ncol - 1)
    def _():
        corner.start()
        beside.start()

    pair.wait_recv()
    acc0[...] = red_ref[core] + got0[...]
    first = []
    for d in range(1, nrow):
        peer = row_peer(d)
        first.append(remote(acc0.at[peer[0]], got1.at[r], send1.at[d], recv1.at[d], peer))
        first[-1].start()

    for b in range(blocks):
        obj_ref[:, :, b * n : (b + 1) * n] = grad_ref[:, b, :height]
    rim[...] = grad_ref[:, 0, height:]

    for one in first:
        one.wait_recv()

    total = acc0[r]
    for d in range(1, nrow):
        total = total + got1[lax.rem(r + nrow - d, nrow)]
    acc1[...] = total

    second = []
    for d in range(1, nchip):
        second.append(remote(acc1, got2.at[chip], send2.at[d], recv2.at[d], chip_peer(d)))
        second[-1].start()
    got2[chip] = total

    @pl.when(c > 0)
    def _():
        corner.wait_recv()
        rim[...] += in_corner[...]

    @pl.when(r < nrow - 1)
    def _():
        for one in below:
            one.start()

    for one in second:
        one.wait_recv()
    total = got2[0]
    for k in range(1, nchip):
        total = total + got2[k]
    every[core, r] = total

    third = []
    for d in range(1, nrow):
        piece = every.at[core, r]
        third.append(remote(piece, piece, send3.at[d], recv3.at[d], row_peer(d)))
        third[-1].start()

    @pl.when(c > 0)
    def _():
        beside.wait_recv()
        obj_ref[:, :, :n] += in_right[...]

    for one in third:
        one.wait_recv()
    fourth = remote(every.at[core], every.at[core], send4.at[0], recv4.at[0], twin)
    fourth.start()

    @pl.when(r > 0)
    def _():
        for b, one in enumerate(below):
            one.wait_recv()
            obj_ref[:, :n, b * n : (b + 1) * n] += in_below[:, b]

    fourth.wait_recv()

    for one in [pair] + first + second + third + [fourth]:
        one.wait_send()

    @pl.when(c < ncol - 1)
    def _():
        corner.wait_send()
        beside.wait_send()

    @pl.when(r < nrow - 1)
    def _():
        for one in below:
            one.wait_send()


def result_kernel(shares, obj_ref, every, object_out, probe_out, probe, sems):
    tiles, half, share = shares
    n = probe.shape[-1]
    per = n // 8
    objects = pltpu.make_async_copy(obj_ref, object_out, sems.at[0])
    objects.start()

    def tile(g):
        k = g % half
        return every[g // half, k // share, k % share]

    for i in range(per):
        factor = lax.rsqrt(tile(4 * per + i) + 1.0)
        for ch in range(4):
            probe[ch // 2, ch % 2, 8 * i : 8 * i + 8] = tile(ch * per + i) * factor
    steps = pltpu.make_async_copy(probe, probe_out, sems.at[1])
    steps.start()
    objects.wait()
    steps.wait()


def per_device(nrow, ncol, tables, object_field, probe_modes, measured, positions, counts):
    n = probe_modes.shape[-1]
    _, height, width = object_field.shape
    blocks, slots = width // n, measured.shape[2]
    shares = tiles, half, share = tiling(nrow, n)
    group = 8 if slots % 8 == 0 else 1
    params = functools.partial(pltpu.CompilerParams, vmem_limit_bytes=LIMIT)
    dma = pltpu.SemaphoreType.DMA
    extended = pl.pallas_call(
        functools.partial(halo_kernel, nrow, ncol, n),
        out_shape=jax.ShapeDtypeStruct((2, blocks + 1, height + n, n), F32),
        in_specs=[HBM],
        out_specs=VMEM,
        scratch_shapes=[dma((blocks + 2,)), dma((blocks + 2,)), dma((blocks,))],
        compiler_params=params(collective_id=0, has_side_effects=True),
    )(object_field)
    gradient, sums = pl.pallas_call(
        functools.partial(compute_kernel, shares, group, height, width),
        out_shape=(
            jax.ShapeDtypeStruct((2, blocks + 1, height + n, n), F32),
            jax.ShapeDtypeStruct((2, nrow, share, 8, n), F32),
        ),
        in_specs=[SMEM, SMEM] + [VMEM] * 5,
        out_specs=(VMEM, VMEM),
        scratch_shapes=[pltpu.VMEM((5, n, n), F32)],
        compiler_params=params(),
    )(positions[0, 0], counts, extended, probe_modes, measured[0, 0], *tables)
    object_new, total = pl.pallas_call(
        functools.partial(finish_kernel, nrow, ncol, n, shares),
        out_shape=(
            jax.ShapeDtypeStruct((2, height, width), F32),
            jax.ShapeDtypeStruct((2, nrow, share, 8, n), F32),
        ),
        in_specs=[VMEM, VMEM],
        out_specs=(VMEM, VMEM),
        scratch_shapes=[
            pltpu.VMEM((nrow, share, 8, n), F32),
            pltpu.VMEM((nrow, share, 8, n), F32),
            pltpu.VMEM((nrow, share, 8, n), F32),
            pltpu.VMEM((share, 8, n), F32),
            pltpu.VMEM((ncol // 2, share, 8, n), F32),
            pltpu.VMEM((2, height, n), F32),
            pltpu.VMEM((2, n, n), F32),
            pltpu.VMEM((2, blocks, n, n), F32),
            pltpu.VMEM((2, n, n), F32),
        ]
        + [dma((k,)) for k in (1, 1, nrow, nrow, ncol // 2, ncol // 2, nrow, nrow, 1, 1, 2 + blocks, 2 + blocks)],
        compiler_params=params(collective_id=1, has_side_effects=True),
    )(gradient, sums)
    return pl.pallas_call(
        functools.partial(result_kernel, shares),
        out_shape=(
            jax.ShapeDtypeStruct((2, height, width), F32),
            jax.ShapeDtypeStruct((2, 2, n, n), F32),
        ),
        in_specs=[VMEM, VMEM],
        out_specs=(HBM, HBM),
        scratch_shapes=[pltpu.VMEM((2, 2, n, n), F32), dma((2,))],
        compiler_params=params(),
    )(object_new, total)


def solution(mesh):
    nrow, ncol = mesh.shape["row"], mesh.shape["col"]
    in_specs = (
        P(None, "row", "col"),
        P(),
        P("row", "col", None, None, None),
        P("row", "col", None, None),
        P("row", "col"),
    )
    out_specs = (P(None, "row", "col"), P())

    def run(object_field, probe_modes, measured, positions, counts):
        tables = [jnp.asarray(t) for t in fourier_tables(probe_modes.shape[-1])]
        return jax.shard_map(
            functools.partial(per_device, nrow, ncol, tables),
            mesh=mesh, in_specs=in_specs, out_specs=out_specs, check_vma=False,
        )(object_field, probe_modes, measured, positions, counts)

    return run
```
